512 devices in a mesh: band: 64 (over z, x_lo, core), ga: 8 (over x_hi, y).
Axes of the slice: x: 4 (x_hi: 2, x_lo: 2; x = x_hi * 2 + x_lo), y: 4, z: 16, core: 2. Of those that a mesh axis runs over, the one named last changes fastest.
Arguments:
- orbitals: bfloat16 [128, 128, 128, 128], P('band', 'ga'), may hold values from -6 to 6
- owners: int32 [2], replicated, may hold values from 0 to 127
- cutoff: int32 [128, 128], replicated, may hold values from 16 to 64
Outputs:
- exchange_terms: float32 [128, 128, 128, 128], P('band', 'ga')
- owner_terms: bfloat16 [2, 128, 128, 128], P(None, 'ga')
The draws below stay inside these ranges and needn't reach their ends.
All inputs are finite; a program needn't handle non-finite values.
Results may differ from the reference program's by a relative error of at most 0.012.
Values may be sent and summed in bfloat16 or wider, within the bound.
No kernel may reach another device: no remote copies, remote signals or barrier semaphores. Data moves between devices by JAX's collectives and lax.ppermute only.
A program may use at most 64 MiB of HBM per device.

```python
import math
import jax
import jax.numpy as jnp
from jax import lax

GRID = 128
STEPS = 2
BANDS = 128


def touch_ends(array, key, low, top_value):
    longest = array.shape.index(max(array.shape))
    spots = []
    for shift in (0, 1):
        where = [jax.random.randint(jax.random.fold_in(key, axis), (), 0, length) for axis, length in enumerate(array.shape)]
        where[longest] = (where[longest] + shift) % array.shape[longest]
        spots.append(tuple(where))
    return array.at[spots[0]].set(low).at[spots[1]].set(top_value)


def levels(stream_key, shape, shards, smallest, top_value):
    gain, own = 1.0, jax.random.fold_in(stream_key, 6)
    for dim, shards_of in shards:
        heights = jnp.exp(jax.random.uniform(jax.random.fold_in(own, dim), (shards_of,), jnp.float32, smallest / len(shards), top_value / len(shards)))
        gain = gain * jnp.repeat(heights, shape[dim] // shards_of).reshape([-1 if axis == dim else 1 for axis in range(len(shape))])
    return gain


def normal_values(own_key, extent, deviation, reach, split=(), kind=jnp.bfloat16):
    level = levels(own_key, extent, split, -0.22, 0.18) if split else 1.0
    result = jax.random.normal(own_key, extent, jnp.float32) * deviation * level
    return jnp.minimum(jnp.maximum(result, -reach), reach).astype(kind)


def setup_inputs(seed: int = 0) -> dict:
    arg_keys = jax.random.split(jax.random.key(seed), 4)
    return {
        "orbitals": normal_values(arg_keys[0], (BANDS, GRID, GRID, GRID), 1.0, 6.0, ((0, 64), (1, 8))),
        "owners": jax.random.randint(arg_keys[1], (STEPS,), 0, BANDS).astype(jnp.int32),
        "cutoff": touch_ends(jax.random.randint(arg_keys[2], (GRID, GRID), GRID // 8, GRID // 2 + 1), jax.random.fold_in(arg_keys[2], 1), GRID // 8, (GRID // 2 + 1) - 1).astype(jnp.int32),
    }


COULOMB = math.pi / 8


def signed_freq(indices, length):
    return jnp.where(indices < length // 2, indices, indices - length)


def symmetric_cutoff(cutoff):
    length = cutoff.shape[0]
    mirror = (length - jnp.arange(length, dtype=jnp.int32)) % length
    mirrored = jnp.take(jnp.take(cutoff, mirror, axis=0), mirror, axis=1)
    return jnp.minimum(cutoff, mirrored)


def coulomb_kernel(limits, first_row):
    length = limits.shape[0]
    rows = limits.shape[1]
    full_range = jnp.arange(length, dtype=jnp.int32)
    freq_full = signed_freq(full_range, length)
    freq_rows = signed_freq(first_row + jnp.arange(rows, dtype=jnp.int32), length)
    squared = (freq_full[:, None, None] ** 2 + freq_rows[None, :, None] ** 2 + freq_full[None, None, :] ** 2).astype(jnp.float32)
    inside = (jnp.abs(freq_full)[None, None, :] <= limits[:, :, None]) & (squared > 0)
    scale = COULOMB * float(length) ** 1.5
    return jnp.where(inside, scale / jnp.maximum(squared, 1.0), 0.0).astype(jnp.float32)


def reference(orbitals, owners, cutoff):
    values = orbitals.astype(jnp.float32)
    kernel = coulomb_kernel(symmetric_cutoff(cutoff), 0)

    def one_step(totals, owner):
        owner_field = lax.dynamic_index_in_dim(values, owner, 0, keepdims=False)

        def solve(band_values):
            density = band_values * owner_field
            spectrum = jnp.fft.fftn(density) * kernel
            return jnp.real(jnp.fft.ifftn(spectrum)).astype(jnp.float32)

        potential = lax.map(solve, values)
        totals = totals + potential * owner_field
        owner_part = jnp.sum(potential * values, axis=0)
        return totals, owner_part

    exchange_terms, owner_parts = lax.scan(one_step, jnp.zeros(values.shape, jnp.float32), owners)
    return exchange_terms, owner_parts.astype(jnp.bfloat16)
```

```python
import math

import jax
import jax.numpy as jnp
import numpy as np
from jax import lax
from jax.experimental import pallas as pl
from jax.experimental.pallas import tpu as pltpu
from jax.sharding import Mesh, PartitionSpec as P

COULOMB = math.pi / 8
GRID = 128
STEPS = 2
ROWS = 16
CHUNK = STEPS * ROWS * 2 * ROWS
BF16 = jnp.bfloat16
F32 = jnp.float32

AXES = ("zh", "zl", "xl", "core", "xh", "y")
SIZES = (8, 2, 2, 2, 2, 4)
GA = ("xh", "y")
QUAD = ("zl", "xl")
VMEM = pl.BlockSpec(memory_space=pltpu.VMEM)


def dft_tables():
    indices = np.arange(GRID)
    angles = (indices[:, None] * indices[None, :] % GRID) * (2.0 * np.pi / GRID)
    cosine, sine = np.cos(angles), np.sin(angles)
    matrix = np.block([[cosine, -sine], [sine, cosine]]).astype(np.float32)
    high = matrix.astype(BF16)
    low = (matrix - high.astype(np.float32)).astype(BF16)
    return np.stack([high, low, high.T, low.T])


def dot(a, b):
    return jnp.dot(a, b, preferred_element_type=F32)


def split(x):
    high = x.astype(BF16)
    return high, (x - high.astype(F32)).astype(BF16)


def right(x, tables, which):
    high, low = split(x)
    return dot(high, tables[which]) + (dot(low, tables[which]) + dot(high, tables[which + 1]))


def left(x, tables, which):
    high, low = split(x)
    return dot(tables[which], high) + (dot(tables[which], low) + dot(tables[which + 1], high))


def left_exact(x, tables, which):
    return dot(tables[which], x) + dot(tables[which + 1], x)


def quarter_swap(x):
    n = GRID
    return jnp.concatenate(
        [
            jnp.concatenate([x[:n, :n], x[n:, :n]], axis=1),
            jnp.concatenate([x[:n, n:], x[n:, n:]], axis=1),
        ],
        axis=0,
    )


def forward_kernel(values, owner, tables, out, scratch):
    n = GRID
    for s in range(STEPS):

        def planes(p, carry):
            field = owner[p // 4, p % 4, :, s].reshape(2 * n, n).astype(F32)
            first = values[0, pl.ds(2 * p, 2)].reshape(2 * n, n).astype(F32)
            second = values[1, pl.ds(2 * p, 2)].reshape(2 * n, n).astype(F32)
            density = jnp.concatenate([first * field, second * field], axis=1)
            along_z = quarter_swap(right(density, tables, 0))
            along_y = left(along_z, tables, 2)
            start = pl.multiple_of(2 * p * n, 2 * n)
            for part in range(2):
                rows = along_y[part * n : (part + 1) * n]
                scratch[2 * s + part, pl.ds(start, n), :] = rows[:, :n]
                scratch[2 * s + part, pl.ds(start + n, n), :] = rows[:, n:]
            return carry

        lax.fori_loop(0, ROWS // 2, planes, 0)

    lane = lax.broadcasted_iota(jnp.int32, (ROWS, n), 1)

    def send(j, carry):
        rest = jnp.zeros((ROWS, n), F32)
        for s in range(STEPS):
            for k in range(ROWS):
                for part in range(2):
                    field = 2 * s + part
                    tile = scratch[field, pl.ds(j * ROWS + k, ROWS, stride=n), :]
                    high = tile.astype(BF16)
                    row = ((s * ROWS + k) * 2 + part) * ROWS
                    out[j, row : row + ROWS] = high
                    if k == 0:
                        low = tile - high.astype(F32)
                        below = low - low.astype(BF16).astype(F32)
                        rest = jnp.where(lane == field, low[:, :1], rest)
                        rest = jnp.where(lane == field + 2 * STEPS, below[:, :1], rest)
        out[j, CHUNK:] = rest.astype(BF16)
        return carry

    lax.fori_loop(0, n // ROWS, send, 0)


def solve_kernel(spectrum, coulomb, tables, out, scratch):
    n = GRID
    rest = spectrum[:, CHUNK:].reshape(n, n).astype(F32)
    lane = lax.broadcasted_iota(jnp.int32, (n, n), 1)
    dropped = coulomb[0, :1, :1] == 0.0
    for s in range(STEPS):

        def pick(k):
            row = pl.multiple_of((s * ROWS + k) * 2 * ROWS, 2 * ROWS)
            return [spectrum[:, pl.ds(row + part * ROWS, ROWS)].reshape(n, n) for part in range(2)]

        def factor(q):
            pair = jnp.concatenate([coulomb[2 * q], coulomb[2 * q + 1]], axis=1)
            return jnp.concatenate([pair, pair], axis=0)

        def keep(q, solved):
            start = pl.multiple_of(q * 4 * n, 4 * n)
            scratch[pl.ds(start, 2 * n), :] = solved[:, :n]
            scratch[pl.ds(start + 2 * n, 2 * n), :] = solved[:, n:]

        def columns(q, carry):
            both = jnp.concatenate(
                [jnp.concatenate(pick(2 * q), axis=0), jnp.concatenate(pick(2 * q + 1), axis=0)],
                axis=1,
            )
            keep(q, left(left_exact(both, tables, 2) * factor(q), tables, 0))
            return carry

        parts = []
        for part, tile in enumerate(pick(0)):
            tile, field = tile.astype(F32), 2 * s + part
            low = rest[:, field : field + 1] + rest[:, field + 2 * STEPS : field + 2 * STEPS + 1]
            column = tile[:, :1] + low
            mean = jnp.sum(column, axis=0, keepdims=True) * (1.0 / n)
            column = column - jnp.where(dropped, mean, 0.0)
            parts.append(jnp.where(lane == 0, column, tile))
        both = jnp.concatenate(
            [jnp.concatenate(parts, axis=0), jnp.concatenate(pick(1), axis=0).astype(F32)], axis=1
        )
        keep(0, left(left(both, tables, 2) * factor(0), tables, 0))
        lax.fori_loop(1, ROWS // 2, columns, 0)

        def send(i, carry):
            for x in range(ROWS):
                for part in range(2):
                    tile = scratch[pl.ds(part * n + i * ROWS + x, ROWS, stride=2 * n), :]
                    out[i, s, x, part] = tile.astype(BF16)
            return carry

        lax.fori_loop(0, n // ROWS, send, 0)


def backward_kernel(solved, values, owner, tables, exchange, terms):
    n = GRID

    def planes(p, carry):
        first = values[0, pl.ds(2 * p, 2)].reshape(2 * n, n).astype(F32)
        second = values[1, pl.ds(2 * p, 2)].reshape(2 * n, n).astype(F32)
        totals = [0.0, 0.0]
        for s in range(STEPS):

            def pick(x):
                return jnp.concatenate(
                    [solved[:, s, x, part].reshape(n, n) for part in range(2)], axis=0
                )

            both = jnp.concatenate([pick(2 * p), pick(2 * p + 1)], axis=1)
            along_y = quarter_swap(left_exact(both, tables, 0))
            potential = right(along_y, tables, 2)
            field = owner[p // 4, p % 4, :, s].reshape(2 * n, n).astype(F32)
            real, imag = potential[:, :n], potential[:, n:]
            totals = [totals[0] + real * field, totals[1] + imag * field]
            term = real * first + imag * second
            terms[p // 4, p % 4, :, s] = term.astype(BF16).reshape(8, 32, n)
        for band in range(2):
            exchange[band, pl.ds(2 * p, 2)] = totals[band].reshape(2, n, n)
        return carry

    lax.fori_loop(0, ROWS // 2, planes, 0)


def call(kernel, outs, scratch, flops):
    return pl.pallas_call(
        kernel,
        out_shape=outs,
        scratch_shapes=scratch,
        compiler_params=pltpu.CompilerParams(vmem_limit_bytes=40 * 1024 * 1024),
        cost_estimate=pl.CostEstimate(flops=flops, bytes_accessed=5 << 20, transcendentals=0),
    )


def exchange_all(x, axes):
    return lax.all_to_all(x, axes, 0, 0, tiled=True)


def gather_all(x, axes, count):
    return exchange_all(jnp.broadcast_to(x[None], (count,) + x.shape), axes)


def pick_source(x, sources):
    return jnp.stack(
        [lax.dynamic_index_in_dim(x[:, s], sources[s], 0, keepdims=False) for s in range(STEPS)]
    )


def spread_owners(orbitals, owners):
    slots, roots = owners % 2, owners // 2
    core, quad, zh = roots % 2, roots // 2 % 4, roots // 8
    rows = ROWS * GRID
    flat = orbitals.reshape(2, rows, GRID)
    picked = pick_source(jnp.stack([flat, flat], 1), slots)
    piece = picked.reshape(STEPS, 2, rows // 2, GRID).swapaxes(0, 1)
    piece = pick_source(exchange_all(piece, "core"), core)
    piece = piece.reshape(STEPS, 4, rows // 8, GRID).swapaxes(0, 1)
    piece = pick_source(exchange_all(piece, QUAD), quad)
    piece = piece.reshape(STEPS, 8, rows // 64, GRID).swapaxes(0, 1)
    piece = pick_source(exchange_all(piece, "zh"), zh)
    piece = gather_all(piece, "zh", 8)
    piece = gather_all(piece, QUAD, 4)
    return lax.all_gather(piece, "core", axis=0, tiled=False)


def total_terms(terms):
    def reduced(x):
        return jnp.sum(x.astype(F32), axis=0).astype(BF16)

    piece = reduced(exchange_all(terms, "core"))
    piece = reduced(exchange_all(piece, QUAD))
    piece = reduced(exchange_all(piece, "zh"))
    piece = gather_all(piece, "zh", 8)
    piece = gather_all(piece, QUAD, 4)
    return lax.all_gather(piece, "core", axis=0, tiled=False)


def coulomb_slab(cutoff, first_row):
    mirrored = jnp.roll(cutoff[::-1, ::-1], (1, 1), (0, 1))
    limits = lax.dynamic_slice_in_dim(jnp.minimum(cutoff, mirrored), first_row, ROWS, 1).T
    full = jnp.arange(GRID, dtype=jnp.int32)
    signed = jnp.where(full < GRID // 2, full, full - GRID)
    own = first_row + jnp.arange(ROWS, dtype=jnp.int32)
    own = jnp.where(own < GRID // 2, own, own - GRID)
    squared = own[:, None, None] ** 2 + signed[None, :, None] ** 2 + signed[None, None, :] ** 2
    inside = (jnp.abs(signed)[None, None, :] <= limits[:, :, None]) & (squared > 0)
    scale = COULOMB * float(GRID) ** 1.5 / float(GRID) ** 3
    return jnp.where(inside, scale / jnp.maximum(squared, 1).astype(F32), 0.0)


def shards(orbitals, owners, cutoff):
    first_row = lax.axis_index(GA) * ROWS
    coulomb = coulomb_slab(cutoff, first_row)
    tables = jnp.asarray(dft_tables())
    owner = spread_owners(orbitals, owners)
    packed = jax.ShapeDtypeStruct((8, STEPS, ROWS, 2, ROWS, GRID), BF16)
    flops = 2 * 2 * STEPS * 3 * 8 * 256**3
    with jax.named_scope("forward_planes"):
        spectrum = call(
            forward_kernel,
            jax.ShapeDtypeStruct((8, CHUNK + ROWS, GRID), BF16),
            [pltpu.VMEM((2 * STEPS, ROWS * GRID, GRID), F32)],
            flops,
        )(orbitals, owner, tables)
    spectrum = exchange_all(spectrum, GA)
    with jax.named_scope("coulomb_solve"):
        solved = call(solve_kernel, packed, [pltpu.VMEM((ROWS * 2 * GRID, GRID), F32)], flops)(
            spectrum, coulomb, tables
        )
    solved = exchange_all(solved, GA)
    with jax.named_scope("backward_planes"):
        exchange, terms = call(
            backward_kernel,
            (
                jax.ShapeDtypeStruct((2, ROWS, GRID, GRID), F32),
                jax.ShapeDtypeStruct((2, 4, 8, STEPS, 32, GRID), BF16),
            ),
            [],
            flops,
        )(solved, orbitals, owner, tables)
    total = total_terms(terms)
    total = jnp.moveaxis(total, 3, 0).reshape(STEPS, ROWS, GRID, GRID)
    return exchange, total


def solution(mesh):
    inner = Mesh(mesh.devices.reshape(SIZES), AXES)
    band, ga = AXES[:4], AXES[4:]
    return jax.shard_map(
        shards,
        mesh=inner,
        in_specs=(P(band, ga, None, None), P(), P()),
        out_specs=(P(band, ga, None, None), P(None, ga, None, None)),
        check_vma=False,
    )
```

```python
import functools
import math

import jax
import jax.numpy as jnp
import numpy as np
from jax import lax
from jax.experimental import pallas as pl
from jax.experimental.pallas import tpu as pltpu
from jax.sharding import Mesh, PartitionSpec as P

COULOMB = math.pi / 8
GRID = 128
STEPS = 2
ROWS = 16
CHUNK = STEPS * ROWS * 2 * ROWS
BF16 = jnp.bfloat16
F32 = jnp.float32

AXES = ("zh", "zl", "xl", "core", "xh", "y")
SIZES = (4, 4, 2, 2, 2, 4)
GA = ("xh", "y")
OCT = ("zl", "xl")
VMEM = pl.BlockSpec(memory_space=pltpu.VMEM)
SMEM = pl.BlockSpec(memory_space=pltpu.SMEM)
HALF = ROWS // 2


def dft_tables():
    indices = np.arange(GRID)
    angles = (indices[:, None] * indices[None, :] % GRID) * (2.0 * np.pi / GRID)
    cosine, sine = np.cos(angles), np.sin(angles)
    matrix = np.block([[cosine, -sine], [sine, cosine]]).astype(np.float32)
    high = matrix.astype(BF16)
    low = (matrix - high.astype(np.float32)).astype(BF16)
    return np.stack([high, low, high.T, low.T])


def dot(a, b):
    return jnp.dot(a, b, preferred_element_type=F32)


def split(x):
    high = x.astype(BF16)
    return high, (x - high.astype(F32)).astype(BF16)


def right(x, tables, which):
    high, low = split(x)
    return dot(high, tables[which]) + (dot(low, tables[which]) + dot(high, tables[which + 1]))


def left(x, tables, which):
    high, low = split(x)
    return dot(tables[which], high) + (dot(tables[which], low) + dot(tables[which + 1], high))


def left_exact(x, tables, which):
    return dot(tables[which], x) + dot(tables[which + 1], x)


def quarter_swap(x):
    n = GRID
    return jnp.concatenate(
        [
            jnp.concatenate([x[:n, :n], x[n:, :n]], axis=1),
            jnp.concatenate([x[:n, n:], x[n:, n:]], axis=1),
        ],
        axis=0,
    )


def halves(core, own, other):
    first = core[0] * HALF
    return [(own, first), (other, HALF - first)]


def forward_kernel(core, values, own, other, tables, out, scratch):
    n = GRID
    for s in range(STEPS):
        for fields, first in halves(core, own, other):
            for p in range(0, HALF, 2):
                field = fields[p : p + 2, s].reshape(2 * n, n).astype(F32)
                pair = pl.ds(first + p, 2)
                left_band = values[0, pair].reshape(2 * n, n).astype(F32)
                right_band = values[1, pair].reshape(2 * n, n).astype(F32)
                density = jnp.concatenate([left_band * field, right_band * field], axis=1)
                along_z = quarter_swap(right(density, tables, 0))
                along_y = left(along_z, tables, 2)
                start = pl.multiple_of((first + p) * n, 2 * n)
                for part in range(2):
                    rows = along_y[part * n : (part + 1) * n]
                    scratch[2 * s + part, pl.ds(start, n), :] = rows[:, :n]
                    scratch[2 * s + part, pl.ds(start + n, n), :] = rows[:, n:]

    lane = lax.broadcasted_iota(jnp.int32, (ROWS, n), 1)

    def send(j, carry):
        rest = jnp.zeros((ROWS, n), F32)
        for s in range(STEPS):
            for k in range(ROWS):
                for part in range(2):
                    field = 2 * s + part
                    tile = scratch[field, pl.ds(j * ROWS + k, ROWS, stride=n), :]
                    high = tile.astype(BF16)
                    row = ((s * ROWS + k) * 2 + part) * ROWS
                    out[j, row : row + ROWS] = high
                    if k == 0:
                        low = tile - high.astype(F32)
                        below = low - low.astype(BF16).astype(F32)
                        rest = jnp.where(lane == field, low[:, :1], rest)
                        rest = jnp.where(lane == field + 2 * STEPS, below[:, :1], rest)
        out[j, CHUNK:] = rest.astype(BF16)
        return carry

    lax.fori_loop(0, n // ROWS, send, 0)


def solve_kernel(spectrum, coulomb, tables, out, scratch):
    n = GRID
    rest = spectrum[:, CHUNK:].reshape(n, n).astype(F32)
    lane = lax.broadcasted_iota(jnp.int32, (n, n), 1)
    dropped = coulomb[0, :1, :1] == 0.0
    for s in range(STEPS):

        def pick(k):
            row = (s * ROWS + k) * 2 * ROWS
            ends = [row + part * ROWS for part in range(2)]
            return [spectrum[:, end : end + ROWS].reshape(n, n) for end in ends]

        def factor(q):
            pair = jnp.concatenate([coulomb[2 * q], coulomb[2 * q + 1]], axis=1)
            return jnp.concatenate([pair, pair], axis=0)

        def keep(q, solved):
            start = q * 4 * n
            scratch[start : start + 2 * n] = solved[:, :n]
            scratch[start + 2 * n : start + 4 * n] = solved[:, n:]

        def columns(q):
            both = jnp.concatenate(
                [jnp.concatenate(pick(2 * q), axis=0), jnp.concatenate(pick(2 * q + 1), axis=0)],
                axis=1,
            )
            keep(q, left(left_exact(both, tables, 2) * factor(q), tables, 0))

        parts = []
        for part, tile in enumerate(pick(0)):
            tile, field = tile.astype(F32), 2 * s + part
            low = rest[:, field : field + 1] + rest[:, field + 2 * STEPS : field + 2 * STEPS + 1]
            column = tile[:, :1] + low
            mean = jnp.sum(column, axis=0, keepdims=True) * (1.0 / n)
            column = column - jnp.where(dropped, mean, 0.0)
            parts.append(jnp.where(lane == 0, column, tile))
        both = jnp.concatenate(
            [jnp.concatenate(parts, axis=0), jnp.concatenate(pick(1), axis=0).astype(F32)], axis=1
        )
        keep(0, left(left(both, tables, 2) * factor(0), tables, 0))
        for q in range(1, ROWS // 2):
            columns(q)

        def send(i, carry):
            for x in range(ROWS):
                for part in range(2):
                    tile = scratch[pl.ds(part * n + i * ROWS + x, ROWS, stride=2 * n), :]
                    out[i, s, x, part] = tile.astype(BF16)
            return carry

        lax.fori_loop(0, n // ROWS, send, 0)


def backward_kernel(core, solved, values, own, other, tables, exchange, keep, send):
    n = GRID
    for (fields, first), terms in zip(halves(core, own, other), (keep, send)):
        for p in range(0, HALF, 2):
            pair = pl.ds(first + p, 2)
            left_band = values[0, pair].reshape(2 * n, n).astype(F32)
            right_band = values[1, pair].reshape(2 * n, n).astype(F32)
            totals = [0.0, 0.0]
            for s in range(STEPS):

                def pick(x):
                    parts = [solved[:, s, x, part].reshape(n, n) for part in range(2)]
                    return jnp.concatenate(parts, axis=0)

                both = jnp.concatenate([pick(first + p), pick(first + p + 1)], axis=1)
                along_y = quarter_swap(left_exact(both, tables, 0))
                potential = right(along_y, tables, 2)
                field = fields[p : p + 2, s].reshape(2 * n, n).astype(F32)
                real, imag = potential[:, :n], potential[:, n:]
                totals = [totals[0] + real * field, totals[1] + imag * field]
                term = real * left_band + imag * right_band
                terms[p : p + 2, s] = term.astype(terms.dtype).reshape(2, n, n)
            for band in range(2):
                exchange[band, pair] = totals[band].reshape(2, n, n)


def pick_slot(owners, orbitals, out):
    for s in range(STEPS):
        slot = lax.rem(owners[s], 2)
        for half in range(2):
            out[half, s] = orbitals[slot, half * HALF : (half + 1) * HALF]


def pick_core(owners, pieces, out):
    for s in range(STEPS):
        core = lax.rem(lax.div(owners[s], 2), 2)
        for x in range(HALF):
            out[x, s] = pieces[core, s, x]


def pick_copies(divisor, count, owners, pieces, out):
    for s in range(STEPS):
        piece = pieces[lax.rem(lax.div(owners[s], divisor), count), s]
        for copy in range(out.shape[0]):
            out[copy, s] = piece


def assemble(core, own, other, out):
    for half, first in halves(core, own, other):
        for s in range(STEPS):
            for x in range(HALF):
                out[s, first + x] = half[x, s]


def call(kernel, outs, scratch, flops, scalars=1, operands=4):
    return pl.pallas_call(
        kernel,
        out_shape=outs,
        in_specs=[SMEM] * scalars + [VMEM] * operands,
        scratch_shapes=scratch,
        compiler_params=pltpu.CompilerParams(vmem_limit_bytes=40 * 1024 * 1024),
        cost_estimate=pl.CostEstimate(flops=flops, bytes_accessed=5 << 20, transcendentals=0),
    )


def exchange_all(x, axes):
    return lax.all_to_all(x, axes, 0, 0, tiled=True)


def gather_all(x, axes, count):
    return exchange_all(jnp.broadcast_to(x[None], (count,) + x.shape), axes)


def swap_cores(x):
    return lax.ppermute(x, "core", [(0, 1), (1, 0)])


def pick(kernel, shape, owners, pieces):
    outs = jax.ShapeDtypeStruct(shape + (GRID, GRID), BF16)
    return call(kernel, outs, [], 1 << 20, operands=1)(owners, pieces)


def spread_owners(orbitals, owners):
    piece = pick(pick_slot, (2, STEPS, HALF), owners, orbitals)
    piece = pick(pick_core, (HALF, STEPS), owners, exchange_all(piece, "core"))
    piece = exchange_all(piece, OCT)
    piece = pick(functools.partial(pick_copies, 4, 8), (4, STEPS), owners, piece)
    piece = exchange_all(piece, "zh")
    piece = pick(functools.partial(pick_copies, 32, 4), (8, STEPS), owners, piece)
    own = exchange_all(piece, OCT)
    return own, swap_cores(own)


def total_terms(keep, send):
    piece = (keep + swap_cores(send).astype(F32)).astype(BF16)
    piece = jnp.sum(exchange_all(piece, OCT).astype(F32), axis=0).astype(BF16)
    piece = gather_all(piece, "zh", 4)
    piece = jnp.sum(piece.astype(F32), axis=0).astype(BF16)
    own = gather_all(piece, OCT, 8)
    return own, swap_cores(own)


def coulomb_slab(cutoff, first_row):
    mirrored = jnp.roll(cutoff[::-1, ::-1], (1, 1), (0, 1))
    limits = lax.dynamic_slice_in_dim(jnp.minimum(cutoff, mirrored), first_row, ROWS, 1).T
    full = jnp.arange(GRID, dtype=jnp.int32)
    signed = jnp.where(full < GRID // 2, full, full - GRID)
    own = first_row + jnp.arange(ROWS, dtype=jnp.int32)
    own = jnp.where(own < GRID // 2, own, own - GRID)
    squared = own[:, None, None] ** 2 + signed[None, :, None] ** 2 + signed[None, None, :] ** 2
    inside = (jnp.abs(signed)[None, None, :] <= limits[:, :, None]) & (squared > 0)
    scale = COULOMB * float(GRID) ** 1.5 / float(GRID) ** 3
    return jnp.where(inside, scale / jnp.maximum(squared, 1).astype(F32), 0.0)


def shards(orbitals, owners, cutoff):
    first_row = lax.axis_index(GA) * ROWS
    coulomb = coulomb_slab(cutoff, first_row)
    tables = jnp.asarray(dft_tables())
    core = lax.axis_index("core").astype(jnp.int32).reshape(1)
    own, other = spread_owners(orbitals, owners)
    flops = 2 * 2 * STEPS * 3 * 8 * 256**3
    with jax.named_scope("forward_planes"):
        spectrum = call(
            forward_kernel,
            jax.ShapeDtypeStruct((8, CHUNK + ROWS, GRID), BF16),
            [pltpu.VMEM((2 * STEPS, ROWS * GRID, GRID), F32)],
            flops,
        )(core, orbitals, own, other, tables)
    spectrum = exchange_all(spectrum, GA)
    with jax.named_scope("coulomb_solve"):
        solved = call(
            solve_kernel,
            jax.ShapeDtypeStruct((8, STEPS, ROWS, 2, ROWS, GRID), BF16),
            [pltpu.VMEM((ROWS * 2 * GRID, GRID), F32)],
            flops,
            scalars=0,
            operands=3,
        )(spectrum, coulomb, tables)
    solved = exchange_all(solved, GA)
    with jax.named_scope("backward_planes"):
        exchange, keep, send = call(
            backward_kernel,
            (
                jax.ShapeDtypeStruct((2, ROWS, GRID, GRID), F32),
                jax.ShapeDtypeStruct((HALF, STEPS, GRID, GRID), F32),
                jax.ShapeDtypeStruct((HALF, STEPS, GRID, GRID), BF16),
            ),
            [],
            flops,
            operands=5,
        )(core, solved, orbitals, own, other, tables)
    own, other = total_terms(keep, send)
    outs = jax.ShapeDtypeStruct((STEPS, ROWS, GRID, GRID), BF16)
    return exchange, call(assemble, outs, [], 1 << 20, operands=2)(core, own, other)


def solution(mesh):
    inner = Mesh(mesh.devices.reshape(SIZES), AXES)
    band, ga = AXES[:4], AXES[4:]
    return jax.shard_map(
        shards,
        mesh=inner,
        in_specs=(P(band, ga, None, None), P(), P()),
        out_specs=(P(band, ga, None, None), P(None, ga, None, None)),
        check_vma=False,
    )
```

```python
import functools
import math

import jax
import jax.numpy as jnp
import numpy as np
from jax import lax
from jax.experimental import pallas as pl
from jax.experimental.pallas import tpu as pltpu
from jax.sharding import PartitionSpec as P

COULOMB = math.pi / 8
GRID = 128
STEPS = 2
ROWS = 16
CHUNK = STEPS * ROWS * 2 * ROWS
BF16 = jnp.bfloat16
F32 = jnp.float32

SHIFT = 2


def place(z, xl, core):
    return z % 16 * 4 + xl * 2 + core


NEAR = [
    [place(4 * k + j + SHIFT * core, xl, core) for j in range(4) for xl in range(2)]
    for core in range(2)
    for k in range(4)
]
FAR = [
    [place(4 * k + j + SHIFT * core, xl, core) for k in range(4)]
    for core in range(2)
    for j in range(4)
    for xl in range(2)
]
CORES = [[2 * i, 2 * i + 1] for i in range(32)]
VMEM = pl.BlockSpec(memory_space=pltpu.VMEM)
SMEM = pl.BlockSpec(memory_space=pltpu.SMEM)
HALF = ROWS // 2


def dft_tables():
    indices = np.arange(GRID)
    angles = (indices[:, None] * indices[None, :] % GRID) * (2.0 * np.pi / GRID)
    cosine, sine = np.cos(angles), np.sin(angles)
    matrix = np.block([[cosine, -sine], [sine, cosine]]).astype(np.float32)
    high = matrix.astype(BF16)
    low = (matrix - high.astype(np.float32)).astype(BF16)
    return np.stack([high, low, high.T, low.T])


def dot(a, b):
    return jnp.dot(a, b, preferred_element_type=F32)


def split(x):
    high = x.astype(BF16)
    return high, (x - high.astype(F32)).astype(BF16)


def right(x, tables, which):
    high, low = split(x)
    return dot(high, tables[which]) + (dot(low, tables[which]) + dot(high, tables[which + 1]))


def right_exact(x, tables, which):
    return dot(x, tables[which]) + dot(x, tables[which + 1])


def left(x, tables, which):
    high, low = split(x)
    return dot(tables[which], high) + (dot(tables[which], low) + dot(tables[which + 1], high))


def left_exact(x, tables, which):
    return dot(tables[which], x) + dot(tables[which + 1], x)


def quarter_swap(x):
    n = GRID
    return jnp.concatenate(
        [
            jnp.concatenate([x[:n, :n], x[n:, :n]], axis=1),
            jnp.concatenate([x[:n, n:], x[n:, n:]], axis=1),
        ],
        axis=0,
    )


def halves(core, own, other):
    first = core[0] * HALF
    return [(own, first), (other, HALF - first)]


def forward_kernel(core, values, own, other, tables, out, scratch):
    n = GRID
    for s in range(STEPS):
        for fields, first in halves(core, own, other):
            for p in range(0, HALF, 2):
                field = fields[p : p + 2, s].reshape(2 * n, n).astype(F32)
                pair = pl.ds(first + p, 2)
                left_band = values[0, pair].reshape(2 * n, n).astype(F32)
                right_band = values[1, pair].reshape(2 * n, n).astype(F32)
                density = jnp.concatenate([left_band * field, right_band * field], axis=1)
                along_z = quarter_swap(right(density, tables, 0))
                along_y = left(along_z, tables, 2)
                start = pl.multiple_of((first + p) * n, 2 * n)
                for part in range(2):
                    rows = along_y[part * n : (part + 1) * n]
                    scratch[2 * s + part, pl.ds(start, n), :] = rows[:, :n]
                    scratch[2 * s + part, pl.ds(start + n, n), :] = rows[:, n:]

    lane = lax.broadcasted_iota(jnp.int32, (ROWS, n), 1)

    def send(j, carry):
        rest = jnp.zeros((ROWS, n), F32)
        for s in range(STEPS):
            for k in range(ROWS):
                for part in range(2):
                    field = 2 * s + part
                    tile = scratch[field, pl.ds(j * ROWS + k, ROWS, stride=n), :]
                    high = tile.astype(BF16)
                    row = ((s * ROWS + k) * 2 + part) * ROWS
                    out[j, row : row + ROWS] = high
                    if k == 0:
                        low = tile - high.astype(F32)
                        below = low - low.astype(BF16).astype(F32)
                        rest = jnp.where(lane == field, low[:, :1], rest)
                        rest = jnp.where(lane == field + 2 * STEPS, below[:, :1], rest)
        out[j, CHUNK:] = rest.astype(BF16)
        return carry

    lax.fori_loop(0, n // ROWS, send, 0)


def solve_kernel(spectrum, coulomb, tables, out, scratch):
    n = GRID
    rest = spectrum[:, CHUNK:].reshape(n, n).astype(F32)
    lane = lax.broadcasted_iota(jnp.int32, (n, n), 1)
    dropped = coulomb[0, :1, :1] == 0.0
    for s in range(STEPS):

        def pick(k):
            row = (s * ROWS + k) * 2 * ROWS
            ends = [row + part * ROWS for part in range(2)]
            return [spectrum[:, end : end + ROWS].reshape(n, n) for end in ends]

        def factor(q):
            pair = jnp.concatenate([coulomb[2 * q], coulomb[2 * q + 1]], axis=1)
            return jnp.concatenate([pair, pair], axis=0)

        def inverse(x):
            return left_exact(x.astype(BF16), tables, 0)

        def keep(q, solved):
            start = q * 4 * n
            scratch[start : start + 2 * n] = solved[:, :n]
            scratch[start + 2 * n : start + 4 * n] = solved[:, n:]

        def columns(q):
            both = jnp.concatenate(
                [jnp.concatenate(pick(2 * q), axis=0), jnp.concatenate(pick(2 * q + 1), axis=0)],
                axis=1,
            )
            keep(q, inverse(left_exact(both, tables, 2) * factor(q)))

        parts = []
        for part, tile in enumerate(pick(0)):
            tile, field = tile.astype(F32), 2 * s + part
            low = rest[:, field : field + 1] + rest[:, field + 2 * STEPS : field + 2 * STEPS + 1]
            column = tile[:, :1] + low
            mean = jnp.sum(column, axis=0, keepdims=True) * (1.0 / n)
            column = column - jnp.where(dropped, mean, 0.0)
            parts.append(jnp.where(lane == 0, column, tile))
        both = jnp.concatenate(
            [jnp.concatenate(parts, axis=0), jnp.concatenate(pick(1), axis=0).astype(F32)], axis=1
        )
        keep(0, inverse(left(both, tables, 2) * factor(0)))
        for q in range(1, ROWS // 2):
            columns(q)

        def send(i, carry):
            for x in range(ROWS):
                for part in range(2):
                    tile = scratch[pl.ds(part * n + i * ROWS + x, ROWS, stride=2 * n), :]
                    out[i, s, x, part] = tile.astype(BF16)
            return carry

        lax.fori_loop(0, n // ROWS, send, 0)


def backward_kernel(core, solved, values, own, other, tables, exchange, keep, send):
    n = GRID
    for (fields, first), terms in zip(halves(core, own, other), (keep, send)):
        for p in range(0, HALF, 2):
            pair = pl.ds(first + p, 2)
            left_band = values[0, pair].reshape(2 * n, n).astype(F32)
            right_band = values[1, pair].reshape(2 * n, n).astype(F32)
            totals = [0.0, 0.0]
            for s in range(STEPS):

                def pick(x):
                    parts = [solved[:, s, x, part].reshape(n, n) for part in range(2)]
                    return jnp.concatenate(parts, axis=0)

                both = jnp.concatenate([pick(first + p), pick(first + p + 1)], axis=1)
                along_y = quarter_swap(left_exact(both, tables, 0))
                potential = right_exact(along_y.astype(BF16), tables, 2)
                field = fields[p : p + 2, s].reshape(2 * n, n).astype(F32)
                real, imag = potential[:, :n], potential[:, n:]
                totals = [totals[0] + real * field, totals[1] + imag * field]
                term = real * left_band + imag * right_band
                terms[p : p + 2, s] = term.astype(terms.dtype).reshape(2, n, n)
            for band in range(2):
                exchange[band, pair] = totals[band].reshape(2, n, n)


def pick_slot(owners, core, orbitals, out):
    for s in range(STEPS):
        slot = lax.rem(owners[s], 2)
        for half in range(2):
            out[half, s] = orbitals[slot, half * HALF : (half + 1) * HALF]


def pick_core(owners, core, pieces, out):
    for s in range(STEPS):
        root = lax.rem(lax.div(owners[s], 2), 2)
        for x in range(HALF):
            out[x, s] = pieces[root, s, x]


def root_z(owner, core):
    return lax.rem(lax.div(owner, 8) + 16 - SHIFT * core, 16)


def pick_near(owners, core, pieces, out):
    for s in range(STEPS):
        z, xl = root_z(owners[s], core[0]), lax.rem(lax.div(owners[s], 4), 2)
        piece = pieces[lax.rem(z, 4) * 2 + xl, s]
        for copy in range(out.shape[0]):
            out[copy, s] = piece


def pick_far(owners, core, pieces, out):
    for s in range(STEPS):
        piece = pieces[lax.div(root_z(owners[s], core[0]), 4), s]
        for copy in range(out.shape[0]):
            out[copy, s] = piece


def assemble(core, own, other, out):
    for half, first in halves(core, own, other):
        for s in range(STEPS):
            for x in range(HALF):
                out[s, first + x] = half[x, s]


def call(kernel, outs, scratch, flops, scalars=1, operands=4):
    return pl.pallas_call(
        kernel,
        out_shape=outs,
        in_specs=[SMEM] * scalars + [VMEM] * operands,
        scratch_shapes=scratch,
        compiler_params=pltpu.CompilerParams(vmem_limit_bytes=40 * 1024 * 1024),
        cost_estimate=pl.CostEstimate(flops=flops, bytes_accessed=5 << 20, transcendentals=0),
    )


def exchange_all(x, groups):
    return lax.all_to_all(x, "band", 0, 0, axis_index_groups=groups, tiled=True)


def gather_all(x, groups):
    return exchange_all(jnp.broadcast_to(x[None], (len(groups[0]),) + x.shape), groups)


def exchange_slabs(x):
    return lax.all_to_all(x, "ga", 0, 0, tiled=True)


def swap_cores(x):
    return lax.ppermute(x, "band", [(i, i ^ 1) for i in range(64)])


def pick(kernel, shape, owners, core, pieces):
    outs = jax.ShapeDtypeStruct(shape + (GRID, GRID), BF16)
    return call(kernel, outs, [], 1 << 20, scalars=2, operands=1)(owners, core, pieces)


def spread_owners(orbitals, owners, core):
    piece = pick(pick_slot, (2, STEPS, HALF), owners, core, orbitals)
    piece = pick(pick_core, (HALF, STEPS), owners, core, exchange_all(piece, CORES))
    piece = pick(pick_near, (4, STEPS), owners, core, exchange_all(piece, NEAR))
    piece = pick(pick_far, (8, STEPS), owners, core, exchange_all(piece, FAR))
    return exchange_all(piece, NEAR)


def total_terms(keep, send):
    piece = (keep + swap_cores(send).astype(F32)).astype(BF16)
    piece = jnp.sum(exchange_all(piece, NEAR).astype(F32), axis=0).astype(BF16)
    piece = jnp.sum(gather_all(piece, FAR).astype(F32), axis=0).astype(BF16)
    own = gather_all(piece, NEAR)
    return own, swap_cores(own)


def coulomb_slab(cutoff, first_row):
    mirrored = jnp.roll(cutoff[::-1, ::-1], (1, 1), (0, 1))
    limits = lax.dynamic_slice_in_dim(jnp.minimum(cutoff, mirrored), first_row, ROWS, 1).T
    full = jnp.arange(GRID, dtype=jnp.int32)
    signed = jnp.where(full < GRID // 2, full, full - GRID)
    own = first_row + jnp.arange(ROWS, dtype=jnp.int32)
    own = jnp.where(own < GRID // 2, own, own - GRID)
    squared = own[:, None, None] ** 2 + signed[None, :, None] ** 2 + signed[None, None, :] ** 2
    inside = (jnp.abs(signed)[None, None, :] <= limits[:, :, None]) & (squared > 0)
    scale = COULOMB * float(GRID) ** 1.5 / float(GRID) ** 3
    return jnp.where(inside, scale / jnp.maximum(squared, 1).astype(F32), 0.0)


def shards(orbitals, owners, cutoff):
    first_row = lax.axis_index("ga") * ROWS
    tables = jnp.asarray(dft_tables())
    core = (lax.axis_index("band") % 2).astype(jnp.int32).reshape(1)
    own = spread_owners(orbitals, owners, core)
    cutoff, first_row, own = lax.optimization_barrier((cutoff, first_row, own))
    other = swap_cores(own)
    coulomb, other = lax.optimization_barrier((coulomb_slab(cutoff, first_row), other))
    flops = 2 * 2 * STEPS * 3 * 8 * 256**3
    with jax.named_scope("forward_planes"):
        spectrum = call(
            forward_kernel,
            jax.ShapeDtypeStruct((8, CHUNK + ROWS, GRID), BF16),
            [pltpu.VMEM((2 * STEPS, ROWS * GRID, GRID), F32)],
            flops,
        )(core, orbitals, own, other, tables)
    spectrum = exchange_slabs(spectrum)
    with jax.named_scope("coulomb_solve"):
        solved = call(
            solve_kernel,
            jax.ShapeDtypeStruct((8, STEPS, ROWS, 2, ROWS, GRID), BF16),
            [pltpu.VMEM((ROWS * 2 * GRID, GRID), F32)],
            flops,
            scalars=0,
            operands=3,
        )(spectrum, coulomb, tables)
    solved = exchange_slabs(solved)
    with jax.named_scope("backward_planes"):
        exchange, keep, send = call(
            backward_kernel,
            (
                jax.ShapeDtypeStruct((2, ROWS, GRID, GRID), F32),
                jax.ShapeDtypeStruct((HALF, STEPS, GRID, GRID), F32),
                jax.ShapeDtypeStruct((HALF, STEPS, GRID, GRID), BF16),
            ),
            [],
            flops,
            operands=5,
        )(core, solved, orbitals, own, other, tables)
    own, other = total_terms(keep, send)
    outs = jax.ShapeDtypeStruct((STEPS, ROWS, GRID, GRID), BF16)
    return exchange, call(assemble, outs, [], 1 << 20, operands=2)(core, own, other)


def solution(mesh):
    return jax.shard_map(
        shards,
        mesh=mesh,
        in_specs=(P("band", "ga", None, None), P(), P()),
        out_specs=(P("band", "ga", None, None), P(None, "ga", None, None)),
        check_vma=False,
    )
```

```python
import functools
import math

import jax
import jax.numpy as jnp
import numpy as np
from jax import lax
from jax.experimental import pallas as pl
from jax.experimental.pallas import tpu as pltpu
from jax.sharding import PartitionSpec as P

COULOMB = math.pi / 8
GRID = 128
STEPS = 2
FIELDS = 2
ROWS = 16
CHUNK = FIELDS * ROWS * 2 * ROWS
BF16 = jnp.bfloat16
F32 = jnp.float32

SHIFT = 2


def place(z, xl, core):
    return z % 16 * 4 + xl * 2 + core


NEAR = [
    [place(4 * k + j + SHIFT * core, xl, core) for j in range(4) for xl in range(2)]
    for core in range(2)
    for k in range(4)
]
FAR = [
    [place(4 * k + j + SHIFT * core, xl, core) for k in range(4)]
    for core in range(2)
    for j in range(4)
    for xl in range(2)
]
CORES = [[2 * i, 2 * i + 1] for i in range(32)]
LINE = [group[xl::2] for group in NEAR for xl in range(2)]
VMEM = pl.BlockSpec(memory_space=pltpu.VMEM)
SMEM = pl.BlockSpec(memory_space=pltpu.SMEM)
HALF = ROWS // 2


def dft_tables():
    indices = np.arange(GRID)
    angles = (indices[:, None] * indices[None, :] % GRID) * (2.0 * np.pi / GRID)
    cosine, sine = np.cos(angles), np.sin(angles)
    matrix = np.block([[cosine, -sine], [sine, cosine]]).astype(np.float32)
    high = matrix.astype(BF16)
    low = (matrix - high.astype(np.float32)).astype(BF16)
    return np.stack([high, low, high.T, low.T])


def dot(a, b):
    return jnp.dot(a, b, preferred_element_type=F32)


def split(x):
    high = x.astype(BF16)
    return high, (x - high.astype(F32)).astype(BF16)


def right(x, tables, which):
    high, low = split(x)
    return dot(high, tables[which]) + (dot(low, tables[which]) + dot(high, tables[which + 1]))


def right_exact(x, tables, which):
    return dot(x, tables[which]) + dot(x, tables[which + 1])


def left(x, tables, which):
    high, low = split(x)
    return dot(tables[which], high) + (dot(tables[which], low) + dot(tables[which + 1], high))


def left_exact(x, tables, which):
    return dot(tables[which], x) + dot(tables[which + 1], x)


def quarter_swap(x):
    n = GRID
    return jnp.concatenate(
        [
            jnp.concatenate([x[:n, :n], x[n:, :n]], axis=1),
            jnp.concatenate([x[:n, n:], x[n:, n:]], axis=1),
        ],
        axis=0,
    )


def halves(core, own, other):
    first = core[0] * HALF
    return [(own, first), (other, HALF - first)]


def forward_kernel(core, ours, theirs, own, other, tables, out, scratch):
    n = GRID
    for f, values in enumerate((ours, theirs)):
        for owner, first in halves(core, own, other):
            for p in range(HALF // 2):
                field = owner[p].reshape(2 * n, n).astype(F32)
                pair = pl.ds(first + 2 * p, 2)
                bands = [values[band, pair].reshape(2 * n, n).astype(F32) for band in range(2)]
                density = jnp.concatenate([band * field for band in bands], axis=1)
                along_z = quarter_swap(right(density, tables, 0))
                along_y = left(along_z, tables, 2)
                start = pl.multiple_of((first + 2 * p) * n, 2 * n)
                for part in range(2):
                    rows = along_y[part * n : (part + 1) * n]
                    scratch[2 * f + part, pl.ds(start, n), :] = rows[:, :n]
                    scratch[2 * f + part, pl.ds(start + n, n), :] = rows[:, n:]

    lane = lax.broadcasted_iota(jnp.int32, (ROWS, n), 1)

    def send(j, carry):
        rest = jnp.zeros((ROWS, n), F32)
        for f in range(FIELDS):
            for k in range(ROWS):
                for part in range(2):
                    field = 2 * f + part
                    tile = scratch[field, pl.ds(j * ROWS + k, ROWS, stride=n), :]
                    high = tile.astype(BF16)
                    row = ((f * ROWS + k) * 2 + part) * ROWS
                    out[j, row : row + ROWS] = high
                    if k == 0:
                        low = tile - high.astype(F32)
                        below = low - low.astype(BF16).astype(F32)
                        rest = jnp.where(lane == field, low[:, :1], rest)
                        rest = jnp.where(lane == field + 2 * FIELDS, below[:, :1], rest)
        out[j, CHUNK:] = rest.astype(BF16)
        return carry

    lax.fori_loop(0, n // ROWS, send, 0)


def solve_kernel(spectrum, coulomb, tables, out, scratch):
    n = GRID
    rest = spectrum[:, CHUNK:].reshape(n, n).astype(F32)
    lane = lax.broadcasted_iota(jnp.int32, (n, n), 1)
    dropped = coulomb[0, :1, :1] == 0.0
    for f in range(FIELDS):

        def pick(k):
            row = (f * ROWS + k) * 2 * ROWS
            ends = [row + part * ROWS for part in range(2)]
            return [spectrum[:, end : end + ROWS].reshape(n, n) for end in ends]

        def factor(q):
            pair = jnp.concatenate([coulomb[2 * q], coulomb[2 * q + 1]], axis=1)
            return jnp.concatenate([pair, pair], axis=0)

        def inverse(x):
            return left_exact(x.astype(BF16), tables, 0)

        def keep(q, solved):
            start = q * 4 * n
            scratch[start : start + 2 * n] = solved[:, :n]
            scratch[start + 2 * n : start + 4 * n] = solved[:, n:]

        def columns(q):
            both = jnp.concatenate(
                [jnp.concatenate(pick(2 * q), axis=0), jnp.concatenate(pick(2 * q + 1), axis=0)],
                axis=1,
            )
            keep(q, inverse(left_exact(both, tables, 2) * factor(q)))

        parts = []
        for part, tile in enumerate(pick(0)):
            tile, field = tile.astype(F32), 2 * f + part
            low = rest[:, field : field + 1] + rest[:, field + 2 * FIELDS : field + 2 * FIELDS + 1]
            column = tile[:, :1] + low
            mean = jnp.sum(column, axis=0, keepdims=True) * (1.0 / n)
            column = column - jnp.where(dropped, mean, 0.0)
            parts.append(jnp.where(lane == 0, column, tile))
        both = jnp.concatenate(
            [jnp.concatenate(parts, axis=0), jnp.concatenate(pick(1), axis=0).astype(F32)], axis=1
        )
        keep(0, inverse(left(both, tables, 2) * factor(0)))
        for q in range(1, ROWS // 2):
            columns(q)

        def send(i, carry):
            for x in range(ROWS):
                for part in range(2):
                    tile = scratch[pl.ds(part * n + i * ROWS + x, ROWS, stride=2 * n), :]
                    out[i, f, x, part] = tile.astype(BF16)
            return carry

        lax.fori_loop(0, n // ROWS, send, 0)


def backward_kernel(core, solved, ours, theirs, own, other, tables, exchange, passed, keep, send):
    n = GRID
    for (owner, first), terms in zip(halves(core, own, other), (keep, send)):
        for p in range(HALF // 2):
            pair = pl.ds(first + 2 * p, 2)
            field = owner[p].reshape(2 * n, n).astype(F32)
            term = 0.0
            for f, (values, shares) in enumerate(((ours, exchange), (theirs, passed))):

                def pick(x):
                    parts = [solved[:, f, x, part].reshape(n, n) for part in range(2)]
                    return jnp.concatenate(parts, axis=0)

                both = jnp.concatenate([pick(first + 2 * p), pick(first + 2 * p + 1)], axis=1)
                along_y = quarter_swap(left_exact(both, tables, 0))
                potential = right_exact(along_y.astype(BF16), tables, 2)
                for band in range(2):
                    part = potential[:, band * n : (band + 1) * n]
                    share = (part * field).astype(shares.dtype)
                    shares[band, pair] = share.reshape(2, n, n)
                    term = term + part * values[band, pair].reshape(2 * n, n).astype(F32)
            terms[p] = term.astype(terms.dtype).reshape(2, n, n)


def pick_slot(owners, core, orbitals, out):
    for s in range(STEPS):
        slot = lax.rem(owners[s], 2)
        for half in range(2):
            out[half, s] = orbitals[slot, half * HALF : (half + 1) * HALF]


def pick_core(owners, core, pieces, out):
    for s in range(STEPS):
        root = lax.rem(lax.div(owners[s], 2), 2)
        for x in range(HALF // 2):
            out[2 * x + s] = pieces[root, s, 2 * x : 2 * x + 2]


def root_z(owner, core):
    return lax.rem(lax.div(owner, 8) + 16 - SHIFT * core, 16)


def pick_near(owners, core, step, pieces, out):
    owner = owners[step[0]]
    z, xl = root_z(owner, core[0]), lax.rem(lax.div(owner, 4), 2)
    piece = pieces[lax.rem(z, 4) * 2 + xl]
    for copy in range(out.shape[0]):
        out[copy] = piece


def pick_far(owners, core, step, pieces, out):
    piece = pieces[lax.div(root_z(owners[step[0]], core[0]), 4)]
    for copy in range(out.shape[0]):
        out[copy] = piece


def assemble(core, own, other, out):
    for half, first in halves(core, own, other):
        for s in range(STEPS):
            for x in range(HALF // 2):
                out[s, pl.ds(first + 2 * x, 2)] = half[2 * x + s]


def call(kernel, outs, scratch, flops, scalars=1, operands=4):
    return pl.pallas_call(
        kernel,
        out_shape=outs,
        in_specs=[SMEM] * scalars + [VMEM] * operands,
        scratch_shapes=scratch,
        compiler_params=pltpu.CompilerParams(vmem_limit_bytes=40 * 1024 * 1024),
        cost_estimate=pl.CostEstimate(flops=flops, bytes_accessed=5 << 20, transcendentals=0),
    )


def exchange_all(x, groups):
    return lax.all_to_all(x, "band", 0, 0, axis_index_groups=groups, tiled=True)


def gather_all(x, groups):
    return exchange_all(jnp.broadcast_to(x[None], (len(groups[0]),) + x.shape), groups)


def exchange_slabs(x):
    return lax.all_to_all(x, "ga", 0, 0, tiled=True)


def swap(x, bit):
    return lax.ppermute(x, "band", [(i, i ^ bit) for i in range(64)])


def pick(kernel, shape, scalars, pieces):
    outs = jax.ShapeDtypeStruct(shape + (GRID, GRID), BF16)
    return call(kernel, outs, [], 1 << 20, scalars=len(scalars), operands=1)(*scalars, pieces)


def spread_owners(orbitals, owners, core, step):
    piece = pick(pick_slot, (2, STEPS, HALF), (owners, core), orbitals)
    piece = lax.all_to_all(piece, "band", 0, 0, axis_index_groups=CORES, tiled=True)
    piece = exchange_all(pick(pick_core, (8, 2), (owners, core), piece), NEAR)
    orbitals, piece = lax.optimization_barrier((orbitals, piece))
    theirs = swap(orbitals, 2)
    piece = exchange_all(pick(pick_near, (4, 2), (owners, core, step), piece), FAR)
    theirs, piece = lax.optimization_barrier((theirs, piece))
    piece = exchange_all(pick(pick_far, (4, 2), (owners, core, step), piece), LINE)
    return theirs, piece


def total_terms(keep, send, passed):
    piece = (keep + swap(send, 1).astype(F32)).astype(BF16)
    piece = jnp.sum(exchange_all(piece, LINE).astype(F32), axis=0).astype(BF16)
    passed, piece = lax.optimization_barrier((passed, piece))
    passed = swap(passed, 2)
    piece = jnp.sum(gather_all(piece, FAR).astype(F32), axis=0).astype(BF16)
    passed, piece = lax.optimization_barrier((passed, piece))
    own = gather_all(piece, NEAR)
    return own, swap(own, 1), passed


def coulomb_slab(cutoff, first_row):
    mirrored = jnp.roll(cutoff[::-1, ::-1], (1, 1), (0, 1))
    limits = lax.dynamic_slice_in_dim(jnp.minimum(cutoff, mirrored), first_row, ROWS, 1).T
    full = jnp.arange(GRID, dtype=jnp.int32)
    signed = jnp.where(full < GRID // 2, full, full - GRID)
    own = first_row + jnp.arange(ROWS, dtype=jnp.int32)
    own = jnp.where(own < GRID // 2, own, own - GRID)
    squared = own[:, None, None] ** 2 + signed[None, :, None] ** 2 + signed[None, None, :] ** 2
    inside = (jnp.abs(signed)[None, None, :] <= limits[:, :, None]) & (squared > 0)
    scale = COULOMB * float(GRID) ** 1.5 / float(GRID) ** 3
    return jnp.where(inside, scale / jnp.maximum(squared, 1).astype(F32), 0.0)


def shards(orbitals, owners, cutoff):
    first_row = lax.axis_index("ga") * ROWS
    tables = jnp.asarray(dft_tables())
    band = lax.axis_index("band")
    core = (band % 2).astype(jnp.int32).reshape(1)
    step = (band // 2 % 2).astype(jnp.int32).reshape(1)
    theirs, own = spread_owners(orbitals, owners, core, step)
    cutoff, first_row, own = lax.optimization_barrier((cutoff, first_row, own))
    other = swap(own, 1)
    coulomb, other = lax.optimization_barrier((coulomb_slab(cutoff, first_row), other))
    flops = 2 * 2 * FIELDS * 3 * 8 * 256**3
    with jax.named_scope("forward_planes"):
        spectrum = call(
            forward_kernel,
            jax.ShapeDtypeStruct((8, CHUNK + ROWS, GRID), BF16),
            [pltpu.VMEM((2 * FIELDS, ROWS * GRID, GRID), F32)],
            flops,
            operands=5,
        )(core, orbitals, theirs, own, other, tables)
    spectrum = exchange_slabs(spectrum)
    with jax.named_scope("coulomb_solve"):
        solved = call(
            solve_kernel,
            jax.ShapeDtypeStruct((8, FIELDS, ROWS, 2, ROWS, GRID), BF16),
            [pltpu.VMEM((ROWS * 2 * GRID, GRID), F32)],
            flops,
            scalars=0,
            operands=3,
        )(spectrum, coulomb, tables)
    solved = exchange_slabs(solved)
    slab = (2, ROWS, GRID, GRID)
    half = (HALF // 2, 2, GRID, GRID)
    with jax.named_scope("backward_planes"):
        exchange, passed, keep, send = call(
            backward_kernel,
            tuple(
                jax.ShapeDtypeStruct(shape, kind)
                for shape, kind in ((slab, F32), (slab, BF16), (half, F32), (half, BF16))
            ),
            [],
            flops,
            operands=6,
        )(core, solved, orbitals, theirs, own, other, tables)
    own, other, passed = total_terms(keep, send, passed)
    outs = jax.ShapeDtypeStruct((STEPS, ROWS, GRID, GRID), BF16)
    total = call(assemble, outs, [], 1 << 20, operands=2)(core, own, other)
    return exchange + passed.astype(F32), total


def solution(mesh):
    return jax.shard_map(
        shards,
        mesh=mesh,
        in_specs=(P("band", "ga", None, None), P(), P()),
        out_specs=(P("band", "ga", None, None), P(None, "ga", None, None)),
        check_vma=False,
    )
```

```python
import functools
import math

import jax
import jax.numpy as jnp
import numpy as np
from jax import lax
from jax.experimental import pallas as pl
from jax.experimental.pallas import tpu as pltpu
from jax.sharding import PartitionSpec as P

COULOMB = math.pi / 8
GRID = 128
STEPS = 2
FIELDS = 2
ROWS = 16
PLANE = GRID + 4
PAIR = 2 * GRID + 4
CHUNK = FIELDS * ROWS * 2 * ROWS
BF16 = jnp.bfloat16
F32 = jnp.float32

SHIFT = 2


def place(z, xl, core):
    return z % 16 * 4 + xl * 2 + core


NEAR = [
    [place(4 * k + j + SHIFT * core, xl, core) for j in range(4) for xl in range(2)]
    for core in range(2)
    for k in range(4)
]
FAR = [
    [place(4 * k + j + SHIFT * core, xl, core) for k in range(4)]
    for core in range(2)
    for j in range(4)
    for xl in range(2)
]
CORES = [[2 * i, 2 * i + 1] for i in range(32)]
LINE = [group[xl::2] for group in NEAR for xl in range(2)]
VMEM = pl.BlockSpec(memory_space=pltpu.VMEM)
SMEM = pl.BlockSpec(memory_space=pltpu.SMEM)
HALF = ROWS // 2


def dft_tables():
    indices = np.arange(GRID)
    angles = (indices[:, None] * indices[None, :] % GRID) * (2.0 * np.pi / GRID)
    cosine, sine = np.cos(angles), np.sin(angles)
    matrix = np.block([[cosine, -sine], [sine, cosine]]).astype(np.float32)
    high = matrix.astype(BF16)
    low = (matrix - high.astype(np.float32)).astype(BF16)
    return np.stack([high, low, high.T, low.T])


def dot(a, b):
    return jnp.dot(a, b, preferred_element_type=F32)


def split(x):
    high = x.astype(BF16)
    return high, (x - high.astype(F32)).astype(BF16)


def right(x, tables, which):
    high, low = split(x)
    return dot(high, tables[which]) + (dot(low, tables[which]) + dot(high, tables[which + 1]))


def right_exact(x, tables, which):
    return dot(x, tables[which]) + dot(x, tables[which + 1])


def left(x, tables, which):
    high, low = split(x)
    return dot(tables[which], high) + (dot(tables[which], low) + dot(tables[which + 1], high))


def left_exact(x, tables, which):
    return dot(tables[which], x) + dot(tables[which + 1], x)


def quarter_swap(x):
    n = GRID
    return jnp.concatenate(
        [
            jnp.concatenate([x[:n, :n], x[n:, :n]], axis=1),
            jnp.concatenate([x[:n, n:], x[n:, n:]], axis=1),
        ],
        axis=0,
    )


def halves(core, own, other):
    first = core[0] * HALF
    return [(own, first), (other, HALF - first)]


def forward_kernel(core, ours, theirs, own, other, tables, out, scratch):
    n = GRID
    for f, values in enumerate((ours, theirs)):
        for owner, first in halves(core, own, other):
            for p in range(HALF // 2):
                field = owner[p].reshape(2 * n, n).astype(F32)
                pair = pl.ds(first + 2 * p, 2)
                bands = [values[band, pair].reshape(2 * n, n).astype(F32) for band in range(2)]
                density = jnp.concatenate([band * field for band in bands], axis=1)
                along_z = quarter_swap(right(density, tables, 0))
                along_y = left(along_z, tables, 2)
                start = pl.multiple_of((first + 2 * p) * PLANE, 8)
                for part in range(2):
                    rows = along_y[part * n : (part + 1) * n]
                    scratch[2 * f + part, pl.ds(start, n), :] = rows[:, :n]
                    scratch[2 * f + part, pl.ds(start + PLANE, n), :] = rows[:, n:]

    lane = lax.broadcasted_iota(jnp.int32, (ROWS, n), 1)

    def send(j, carry):
        rest = jnp.zeros((ROWS, n), F32)
        for f in range(FIELDS):
            for k in range(ROWS):
                for part in range(2):
                    field = 2 * f + part
                    tile = scratch[field, pl.ds(j * ROWS + k, ROWS, stride=PLANE), :]
                    high = tile.astype(BF16)
                    row = ((f * ROWS + k) * 2 + part) * ROWS
                    out[j, row : row + ROWS] = high
                    if k == 0:
                        low = tile - high.astype(F32)
                        below = low - low.astype(BF16).astype(F32)
                        rest = jnp.where(lane == field, low[:, :1], rest)
                        rest = jnp.where(lane == field + 2 * FIELDS, below[:, :1], rest)
        out[j, CHUNK:] = rest.astype(BF16)
        return carry

    lax.fori_loop(0, n // ROWS, send, 0)


def solve_kernel(spectrum, coulomb, tables, out, scratch):
    n = GRID
    rest = spectrum[:, CHUNK:].reshape(n, n).astype(F32)
    lane = lax.broadcasted_iota(jnp.int32, (n, n), 1)
    dropped = coulomb[0, :1, :1] == 0.0
    for f in range(FIELDS):

        def pick(k):
            row = (f * ROWS + k) * 2 * ROWS
            ends = [row + part * ROWS for part in range(2)]
            return [spectrum[:, end : end + ROWS].reshape(n, n) for end in ends]

        def factor(q):
            pair = jnp.concatenate([coulomb[2 * q], coulomb[2 * q + 1]], axis=1)
            return jnp.concatenate([pair, pair], axis=0)

        def inverse(x):
            return left_exact(x.astype(BF16), tables, 0)

        def keep(q, solved):
            start = q * 2 * PAIR
            scratch[start : start + 2 * n] = solved[:, :n]
            scratch[start + PAIR : start + PAIR + 2 * n] = solved[:, n:]

        def columns(q):
            both = jnp.concatenate(
                [jnp.concatenate(pick(2 * q), axis=0), jnp.concatenate(pick(2 * q + 1), axis=0)],
                axis=1,
            )
            keep(q, inverse(left_exact(both, tables, 2) * factor(q)))

        parts = []
        for part, tile in enumerate(pick(0)):
            tile, field = tile.astype(F32), 2 * f + part
            low = rest[:, field : field + 1] + rest[:, field + 2 * FIELDS : field + 2 * FIELDS + 1]
            column = tile[:, :1] + low
            mean = jnp.sum(column, axis=0, keepdims=True) * (1.0 / n)
            column = column - jnp.where(dropped, mean, 0.0)
            parts.append(jnp.where(lane == 0, column, tile))
        both = jnp.concatenate(
            [jnp.concatenate(parts, axis=0), jnp.concatenate(pick(1), axis=0).astype(F32)], axis=1
        )
        keep(0, inverse(left(both, tables, 2) * factor(0)))
        for q in range(1, ROWS // 2):
            columns(q)

        def send(i, carry):
            for x in range(ROWS):
                for part in range(2):
                    tile = scratch[pl.ds(part * n + i * ROWS + x, ROWS, stride=PAIR), :]
                    out[i, f, x, part] = tile.astype(BF16)
            return carry

        lax.fori_loop(0, n // ROWS, send, 0)


def backward_kernel(core, solved, ours, theirs, own, other, tables, exchange, passed, keep, send):
    n = GRID
    for (owner, first), terms in zip(halves(core, own, other), (keep, send)):
        for p in range(HALF // 2):
            pair = pl.ds(first + 2 * p, 2)
            field = owner[p].reshape(2 * n, n).astype(F32)
            term = 0.0
            for f, (values, shares) in enumerate(((ours, exchange), (theirs, passed))):

                def pick(x):
                    parts = [solved[:, f, x, part].reshape(n, n) for part in range(2)]
                    return jnp.concatenate(parts, axis=0)

                both = jnp.concatenate([pick(first + 2 * p), pick(first + 2 * p + 1)], axis=1)
                along_y = quarter_swap(left_exact(both, tables, 0))
                potential = right_exact(along_y.astype(BF16), tables, 2)
                for band in range(2):
                    part = potential[:, band * n : (band + 1) * n]
                    share = (part * field).astype(shares.dtype)
                    shares[band, pair] = share.reshape(2, n, n)
                    term = term + part * values[band, pair].reshape(2 * n, n).astype(F32)
            terms[p] = term.astype(terms.dtype).reshape(2, n, n)


def pick_slot(owners, core, step, first_row, orbitals, out, sems):
    copies = []
    for s in range(STEPS):
        slot = lax.rem(owners[s], 2)
        for half in range(2):
            piece = orbitals.at[slot, pl.ds(half * HALF, HALF)]
            copies.append(pltpu.make_async_copy(piece, out.at[half, s], sems.at[s, half]))
            copies[-1].start()
    for copy in copies:
        copy.wait()


def pick_core(owners, core, pieces, out):
    for s in range(STEPS):
        root = lax.rem(lax.div(owners[s], 2), 2)
        for x in range(HALF // 2):
            out[2 * x + s] = pieces[root, s, 2 * x : 2 * x + 2]


def root_z(owner, core):
    return lax.rem(lax.div(owner, 8) + 16 - SHIFT * core, 16)


def pick_near(owners, core, step, pieces, out):
    owner = owners[step[0]]
    z, xl = root_z(owner, core[0]), lax.rem(lax.div(owner, 4), 2)
    piece = pieces[lax.rem(z, 4) * 2 + xl]
    for copy in range(out.shape[0]):
        out[copy] = piece


def pick_far(owners, core, step, pieces, out):
    piece = pieces[lax.div(root_z(owners[step[0]], core[0]), 4)]
    for copy in range(out.shape[0]):
        out[copy] = piece


def assemble(core, own, other, out):
    for half, first in halves(core, own, other):
        for s in range(STEPS):
            for x in range(HALF // 2):
                out[s, pl.ds(first + 2 * x, 2)] = half[2 * x + s]


def call(kernel, outs, scratch, flops, scalars=1, operands=4):
    return pl.pallas_call(
        kernel,
        out_shape=outs,
        in_specs=[SMEM] * scalars + [VMEM] * operands,
        scratch_shapes=scratch,
        compiler_params=pltpu.CompilerParams(vmem_limit_bytes=20 * 1024 * 1024),
        cost_estimate=pl.CostEstimate(flops=flops, bytes_accessed=5 << 20, transcendentals=0),
    )


def exchange_all(x, groups):
    return lax.all_to_all(x, "band", 0, 0, axis_index_groups=groups, tiled=True)


def gather_all(x, groups):
    return exchange_all(jnp.broadcast_to(x[None], (len(groups[0]),) + x.shape), groups)


def exchange_slabs(x):
    return lax.all_to_all(x, "ga", 0, 0, tiled=True)


def swap(x, bit):
    return lax.ppermute(x, "band", [(i, i ^ bit) for i in range(64)])


def pick(kernel, shape, scalars, pieces):
    outs = jax.ShapeDtypeStruct(shape + (GRID, GRID), BF16)
    return call(kernel, outs, [], 1 << 20, scalars=len(scalars), operands=1)(*scalars, pieces)


def spread_owners(orbitals, owners, core, step, first_row):
    piece = pl.pallas_call(
        pick_slot,
        out_shape=jax.ShapeDtypeStruct((2, STEPS, HALF, GRID, GRID), BF16),
        in_specs=[SMEM] * 4 + [pl.BlockSpec(memory_space=pl.ANY)],
        out_specs=VMEM,
        scratch_shapes=[pltpu.SemaphoreType.DMA((STEPS, 2))],
        compiler_params=pltpu.CompilerParams(vmem_limit_bytes=20 * 1024 * 1024),
    )(owners, core, step, first_row.reshape(1), orbitals)
    piece = lax.all_to_all(piece, "band", 0, 0, axis_index_groups=CORES, tiled=True)
    piece = exchange_all(pick(pick_core, (8, 2), (owners, core), piece), NEAR)
    orbitals, piece = lax.optimization_barrier((orbitals, piece))
    theirs = swap(orbitals, 2)
    piece = exchange_all(pick(pick_near, (4, 2), (owners, core, step), piece), FAR)
    theirs, piece = lax.optimization_barrier((theirs, piece))
    piece = exchange_all(pick(pick_far, (4, 2), (owners, core, step), piece), LINE)
    return theirs, piece


def total_terms(keep, send, passed):
    piece = (keep + swap(send, 1).astype(F32)).astype(BF16)
    piece = jnp.sum(exchange_all(piece, LINE).astype(F32), axis=0).astype(BF16)
    passed, piece = lax.optimization_barrier((passed, piece))
    passed = swap(passed, 2)
    piece = jnp.sum(gather_all(piece, FAR).astype(F32), axis=0).astype(BF16)
    passed, piece = lax.optimization_barrier((passed, piece))
    own = gather_all(piece, NEAR)
    return own, swap(own, 1), passed


def coulomb_slab(cutoff, first_row):
    mirrored = jnp.roll(cutoff[::-1, ::-1], (1, 1), (0, 1))
    limits = lax.dynamic_slice_in_dim(jnp.minimum(cutoff, mirrored), first_row, ROWS, 1).T
    signed = np.arange(GRID, dtype=np.int32)
    signed = np.where(signed < GRID // 2, signed, signed - GRID).astype(np.int32)
    own = first_row + np.arange(ROWS, dtype=np.int32)
    own = jnp.where(own < GRID // 2, own, own - GRID)
    squared = own[:, None, None] ** 2 + signed[None, :, None] ** 2 + signed[None, None, :] ** 2
    inside = (np.abs(signed)[None, None, :] <= limits[:, :, None]) & (squared > 0)
    scale = COULOMB * float(GRID) ** 1.5 / float(GRID) ** 3
    return jnp.where(inside, scale / jnp.maximum(squared, 1).astype(F32), 0.0)


def shards(orbitals, owners, cutoff):
    first_row = (lax.axis_index("ga") * ROWS).astype(jnp.int32)
    tables = jnp.asarray(dft_tables())
    band = lax.axis_index("band")
    core = (band % 2).astype(jnp.int32).reshape(1)
    step = (band // 2 % 2).astype(jnp.int32).reshape(1)
    theirs, own = spread_owners(orbitals, owners, core, step, first_row)
    cutoff, first_row, own = lax.optimization_barrier((cutoff, first_row, own))
    other = swap(own, 1)
    coulomb, other = lax.optimization_barrier((coulomb_slab(cutoff, first_row), other))
    flops = 2 * 2 * FIELDS * 3 * 8 * 256**3
    with jax.named_scope("forward_planes"):
        spectrum = call(
            forward_kernel,
            jax.ShapeDtypeStruct((8, CHUNK + ROWS, GRID), BF16),
            [pltpu.VMEM((2 * FIELDS, ROWS * PLANE, GRID), F32)],
            flops,
            operands=5,
        )(core, orbitals, theirs, own, other, tables)
    spectrum = exchange_slabs(spectrum)
    with jax.named_scope("coulomb_solve"):
        solved = call(
            solve_kernel,
            jax.ShapeDtypeStruct((8, FIELDS, ROWS, 2, ROWS, GRID), BF16),
            [pltpu.VMEM((ROWS * PAIR, GRID), F32)],
            flops,
            scalars=0,
            operands=3,
        )(spectrum, coulomb, tables)
    solved = exchange_slabs(solved)
    slab = (2, ROWS, GRID, GRID)
    half = (HALF // 2, 2, GRID, GRID)
    with jax.named_scope("backward_planes"):
        exchange, passed, keep, send = call(
            backward_kernel,
            tuple(
                jax.ShapeDtypeStruct(shape, kind)
                for shape, kind in ((slab, F32), (slab, BF16), (half, F32), (half, BF16))
            ),
            [],
            flops,
            operands=6,
        )(core, solved, orbitals, theirs, own, other, tables)
    own, other, passed = total_terms(keep, send, passed)
    outs = jax.ShapeDtypeStruct((STEPS, ROWS, GRID, GRID), BF16)
    total = call(assemble, outs, [], 1 << 20, operands=2)(core, own, other)
    return exchange + passed.astype(F32), total


def solution(mesh):
    return jax.shard_map(
        shards,
        mesh=mesh,
        in_specs=(P("band", "ga", None, None), P(), P()),
        out_specs=(P("band", "ga", None, None), P(None, "ga", None, None)),
        check_vma=False,
    )
```

```python
import functools
import math

import jax
import jax.numpy as jnp
import numpy as np
from jax import lax
from jax.experimental import pallas as pl
from jax.experimental.pallas import tpu as pltpu
from jax.sharding import PartitionSpec as P

COULOMB = math.pi / 8
GRID = 128
STEPS = 2
FIELDS = 2
ROWS = 16
PLANE = GRID + 4
PAIR = 2 * GRID + 4
CHUNK = FIELDS * ROWS * 2 * ROWS
BF16 = jnp.bfloat16
F32 = jnp.float32

SHIFT = 2


def place(z, xl, core):
    return z % 16 * 4 + xl * 2 + core


def near_z(k, j, core):
    return 4 * k + (j + core) % 4 + SHIFT * core


NEAR = [
    [place(near_z(k, j, core), xl, core) for j in range(4) for xl in range(2)]
    for core in range(2)
    for k in range(4)
]
FAR = [
    [place(4 * quarter + z, xl, core) for quarter in (0, 1, 3, 2)]
    for core in range(2)
    for z in range(4)
    for xl in range(2)
]
CORES = [[2 * i, 2 * i + 1] for i in range(32)]
LINE = [group[xl::2] for group in NEAR for xl in range(2)]
VMEM = pl.BlockSpec(memory_space=pltpu.VMEM)
SMEM = pl.BlockSpec(memory_space=pltpu.SMEM)
HALF = ROWS // 2


def dft_tables():
    indices = np.arange(GRID)
    angles = (indices[:, None] * indices[None, :] % GRID) * (2.0 * np.pi / GRID)
    cosine, sine = np.cos(angles), np.sin(angles)
    matrix = np.block([[cosine, -sine], [sine, cosine]]).astype(np.float32)
    high = matrix.astype(BF16)
    low = (matrix - high.astype(np.float32)).astype(BF16)
    return np.stack([high, low, high.T, low.T])


def dot(a, b):
    return jnp.dot(a, b, preferred_element_type=F32)


def split(x):
    high = x.astype(BF16)
    return high, (x - high.astype(F32)).astype(BF16)


def right(x, tables, which):
    high, low = split(x)
    return dot(high, tables[which]) + (dot(low, tables[which]) + dot(high, tables[which + 1]))


def right_exact(x, tables, which):
    return dot(x, tables[which]) + dot(x, tables[which + 1])


def left(x, tables, which):
    high, low = split(x)
    return dot(tables[which], high) + (dot(tables[which], low) + dot(tables[which + 1], high))


def left_exact(x, tables, which):
    return dot(tables[which], x) + dot(tables[which + 1], x)


def quarter_swap(x):
    n = GRID
    return jnp.concatenate(
        [
            jnp.concatenate([x[:n, :n], x[n:, :n]], axis=1),
            jnp.concatenate([x[:n, n:], x[n:, n:]], axis=1),
        ],
        axis=0,
    )


def halves(core, own, other):
    first = core[0] * HALF
    return [(own, first), (other, HALF - first)]


def forward_kernel(core, ours, theirs, own, other, tables, out, scratch):
    n = GRID
    for f, values in enumerate((ours, theirs)):
        for owner, first in halves(core, own, other):
            for p in range(HALF // 2):
                field = owner[p].reshape(2 * n, n).astype(F32)
                pair = pl.ds(first + 2 * p, 2)
                bands = [values[band, pair].reshape(2 * n, n).astype(F32) for band in range(2)]
                density = jnp.concatenate([band * field for band in bands], axis=1)
                along_z = quarter_swap(right(density, tables, 0))
                along_y = left(along_z, tables, 2)
                start = pl.multiple_of((first + 2 * p) * PLANE, 8)
                for part in range(2):
                    rows = along_y[part * n : (part + 1) * n]
                    scratch[2 * f + part, pl.ds(start, n), :] = rows[:, :n]
                    scratch[2 * f + part, pl.ds(start + PLANE, n), :] = rows[:, n:]

    lane = lax.broadcasted_iota(jnp.int32, (ROWS, n), 1)

    def send(j, carry):
        rest = jnp.zeros((ROWS, n), F32)
        for f in range(FIELDS):
            for k in range(ROWS):
                for part in range(2):
                    field = 2 * f + part
                    tile = scratch[field, pl.ds(j * ROWS + k, ROWS, stride=PLANE), :]
                    high = tile.astype(BF16)
                    row = ((f * ROWS + k) * 2 + part) * ROWS
                    out[j, row : row + ROWS] = high
                    if k == 0:
                        low = tile - high.astype(F32)
                        below = low - low.astype(BF16).astype(F32)
                        rest = jnp.where(lane == field, low[:, :1], rest)
                        rest = jnp.where(lane == field + 2 * FIELDS, below[:, :1], rest)
        out[j, CHUNK:] = rest.astype(BF16)
        return carry

    lax.fori_loop(0, n // ROWS, send, 0)


def solve_kernel(spectrum, coulomb, tables, out, scratch):
    n = GRID
    rest = spectrum[:, CHUNK:].reshape(n, n).astype(F32)
    lane = lax.broadcasted_iota(jnp.int32, (n, n), 1)
    dropped = coulomb[0, :1, :1] == 0.0
    for f in range(FIELDS):

        def pick(k):
            row = (f * ROWS + k) * 2 * ROWS
            ends = [row + part * ROWS for part in range(2)]
            return [spectrum[:, end : end + ROWS].reshape(n, n) for end in ends]

        def factor(q):
            pair = jnp.concatenate([coulomb[2 * q], coulomb[2 * q + 1]], axis=1)
            return jnp.concatenate([pair, pair], axis=0)

        def inverse(x):
            return left_exact(x.astype(BF16), tables, 0)

        def keep(q, solved):
            start = q * 2 * PAIR
            scratch[start : start + 2 * n] = solved[:, :n]
            scratch[start + PAIR : start + PAIR + 2 * n] = solved[:, n:]

        def columns(q):
            both = jnp.concatenate(
                [jnp.concatenate(pick(2 * q), axis=0), jnp.concatenate(pick(2 * q + 1), axis=0)],
                axis=1,
            )
            keep(q, inverse(left_exact(both, tables, 2) * factor(q)))

        parts = []
        for part, tile in enumerate(pick(0)):
            tile, field = tile.astype(F32), 2 * f + part
            low = rest[:, field : field + 1] + rest[:, field + 2 * FIELDS : field + 2 * FIELDS + 1]
            column = tile[:, :1] + low
            mean = jnp.sum(column, axis=0, keepdims=True) * (1.0 / n)
            column = column - jnp.where(dropped, mean, 0.0)
            parts.append(jnp.where(lane == 0, column, tile))
        both = jnp.concatenate(
            [jnp.concatenate(parts, axis=0), jnp.concatenate(pick(1), axis=0).astype(F32)], axis=1
        )
        keep(0, inverse(left(both, tables, 2) * factor(0)))
        for q in range(1, ROWS // 2):
            columns(q)

        def send(i, carry):
            for x in range(ROWS):
                for part in range(2):
                    tile = scratch[pl.ds(part * n + i * ROWS + x, ROWS, stride=PAIR), :]
                    out[i, f, x, part] = tile.astype(BF16)
            return carry

        lax.fori_loop(0, n // ROWS, send, 0)


def backward_kernel(core, solved, ours, theirs, own, other, tables, exchange, passed, keep, send):
    n = GRID
    for (owner, first), terms in zip(halves(core, own, other), (keep, send)):
        for p in range(HALF // 2):
            pair = pl.ds(first + 2 * p, 2)
            field = owner[p].reshape(2 * n, n).astype(F32)
            term = 0.0
            for f, (values, shares) in enumerate(((ours, exchange), (theirs, passed))):

                def pick(x):
                    parts = [solved[:, f, x, part].reshape(n, n) for part in range(2)]
                    return jnp.concatenate(parts, axis=0)

                both = jnp.concatenate([pick(first + 2 * p), pick(first + 2 * p + 1)], axis=1)
                along_y = quarter_swap(left_exact(both, tables, 0))
                potential = right_exact(along_y.astype(BF16), tables, 2)
                for band in range(2):
                    part = potential[:, band * n : (band + 1) * n]
                    share = (part * field).astype(shares.dtype)
                    shares[band, pair] = share.reshape(2, n, n)
                    term = term + part * values[band, pair].reshape(2 * n, n).astype(F32)
            terms[p] = term.astype(terms.dtype).reshape(2, n, n)


def pick_slot(owners, core, step, carry, first_row, orbitals, out, sems):
    copies = []
    for s in range(STEPS):
        slot = lax.rem(owners[s], 2)
        for half in range(2):
            piece = orbitals.at[slot, pl.ds(half * HALF, HALF)]
            copies.append(pltpu.make_async_copy(piece, out.at[half, s], sems.at[s, half]))
            copies[-1].start()
    for copy in copies:
        copy.wait()


def pick_core(owners, core, pieces, out):
    for s in range(STEPS):
        root = lax.rem(lax.div(owners[s], 2), 2)
        for x in range(HALF // 2):
            out[2 * x + s] = pieces[root, s, 2 * x : 2 * x + 2]


def root_z(owner, core):
    return lax.rem(lax.div(owner, 8) + 16 - SHIFT * core, 16)


def pick_near(owners, core, step, pieces, out):
    owner = owners[step[0]]
    z, xl = root_z(owner, core[0]), lax.rem(lax.div(owner, 4), 2)
    piece = pieces[lax.rem(lax.rem(z, 4) + 4 - core[0], 4) * 2 + xl]
    for copy in range(out.shape[0]):
        out[copy] = piece


def pick_far(owners, core, step, carry, pieces, out):
    quarter = lax.rem(lax.div(root_z(owners[step[0]], core[0]), 4) + carry[0], 4)
    piece = pieces[quarter + jnp.where(quarter == 2, 1, 0) - jnp.where(quarter == 3, 1, 0)]
    for copy in range(out.shape[0]):
        out[copy] = piece


def assemble(core, own, other, out):
    for half, first in halves(core, own, other):
        for s in range(STEPS):
            for x in range(HALF // 2):
                out[s, pl.ds(first + 2 * x, 2)] = half[2 * x + s]


def call(kernel, outs, scratch, flops, scalars=1, operands=4):
    return pl.pallas_call(
        kernel,
        out_shape=outs,
        in_specs=[SMEM] * scalars + [VMEM] * operands,
        scratch_shapes=scratch,
        compiler_params=pltpu.CompilerParams(vmem_limit_bytes=20 * 1024 * 1024),
        cost_estimate=pl.CostEstimate(flops=flops, bytes_accessed=5 << 20, transcendentals=0),
    )


def exchange_all(x, groups):
    return lax.all_to_all(x, "band", 0, 0, axis_index_groups=groups, tiled=True)


def gather_all(x, groups):
    return exchange_all(jnp.broadcast_to(x[None], (len(groups[0]),) + x.shape), groups)


def exchange_slabs(x):
    return lax.all_to_all(x, "ga", 0, 0, tiled=True)


def swap(x, bit):
    return lax.ppermute(x, "band", [(i, i ^ bit) for i in range(64)])


def pick(kernel, shape, scalars, pieces):
    outs = jax.ShapeDtypeStruct(shape + (GRID, GRID), BF16)
    return call(kernel, outs, [], 1 << 20, scalars=len(scalars), operands=1)(*scalars, pieces)


def spread_owners(orbitals, owners, core, step, carry, first_row):
    piece = pl.pallas_call(
        pick_slot,
        out_shape=jax.ShapeDtypeStruct((2, STEPS, HALF, GRID, GRID), BF16),
        in_specs=[SMEM] * 5 + [pl.BlockSpec(memory_space=pl.ANY)],
        out_specs=VMEM,
        scratch_shapes=[pltpu.SemaphoreType.DMA((STEPS, 2))],
        compiler_params=pltpu.CompilerParams(vmem_limit_bytes=20 * 1024 * 1024),
    )(owners, core, step, carry, first_row.reshape(1), orbitals)
    piece = lax.all_to_all(piece, "band", 0, 0, axis_index_groups=CORES, tiled=True)
    piece = exchange_all(pick(pick_core, (8, 2), (owners, core), piece), NEAR)
    orbitals, piece = lax.optimization_barrier((orbitals, piece))
    theirs = swap(orbitals, 2)
    piece = exchange_all(pick(pick_near, (4, 2), (owners, core, step), piece), FAR)
    theirs, piece = lax.optimization_barrier((theirs, piece))
    piece = exchange_all(pick(pick_far, (4, 2), (owners, core, step, carry), piece), LINE)
    return theirs, piece


def total_terms(keep, send, passed):
    piece = (keep + swap(send, 1).astype(F32)).astype(BF16)
    piece = jnp.sum(exchange_all(piece, LINE).astype(F32), axis=0).astype(BF16)
    passed, piece = lax.optimization_barrier((passed, piece))
    passed = swap(passed, 2)
    piece = jnp.sum(gather_all(piece, FAR).astype(F32), axis=0).astype(BF16)
    passed, piece = lax.optimization_barrier((passed, piece))
    own = gather_all(piece, NEAR)
    return own, swap(own, 1), passed


def coulomb_slab(cutoff, first_row):
    mirrored = jnp.roll(cutoff[::-1, ::-1], (1, 1), (0, 1))
    limits = lax.dynamic_slice_in_dim(jnp.minimum(cutoff, mirrored), first_row, ROWS, 1).T
    signed = np.arange(GRID, dtype=np.int32)
    signed = np.where(signed < GRID // 2, signed, signed - GRID).astype(np.int32)
    own = first_row + np.arange(ROWS, dtype=np.int32)
    own = jnp.where(own < GRID // 2, own, own - GRID)
    squared = own[:, None, None] ** 2 + signed[None, :, None] ** 2 + signed[None, None, :] ** 2
    inside = (np.abs(signed)[None, None, :] <= limits[:, :, None]) & (squared > 0)
    scale = COULOMB * float(GRID) ** 1.5 / float(GRID) ** 3
    return jnp.where(inside, scale / jnp.maximum(squared, 1).astype(F32), 0.0)


def shards(orbitals, owners, cutoff):
    first_row = (lax.axis_index("ga") * ROWS).astype(jnp.int32)
    tables = jnp.asarray(dft_tables())
    band = lax.axis_index("band")
    core = (band % 2).astype(jnp.int32).reshape(1)
    step = (band // 2 % 2).astype(jnp.int32).reshape(1)
    carry = jnp.where((band % 2 == 1) & (band // 4 % 4 < SHIFT), 1, 0).astype(jnp.int32).reshape(1)
    theirs, own = spread_owners(orbitals, owners, core, step, carry, first_row)
    cutoff, first_row, own = lax.optimization_barrier((cutoff, first_row, own))
    other = swap(own, 1)
    coulomb, other = lax.optimization_barrier((coulomb_slab(cutoff, first_row), other))
    flops = 2 * 2 * FIELDS * 3 * 8 * 256**3
    with jax.named_scope("forward_planes"):
        spectrum = call(
            forward_kernel,
            jax.ShapeDtypeStruct((8, CHUNK + ROWS, GRID), BF16),
            [pltpu.VMEM((2 * FIELDS, ROWS * PLANE, GRID), F32)],
            flops,
            operands=5,
        )(core, orbitals, theirs, own, other, tables)
    spectrum = exchange_slabs(spectrum)
    with jax.named_scope("coulomb_solve"):
        solved = call(
            solve_kernel,
            jax.ShapeDtypeStruct((8, FIELDS, ROWS, 2, ROWS, GRID), BF16),
            [pltpu.VMEM((ROWS * PAIR, GRID), F32)],
            flops,
            scalars=0,
            operands=3,
        )(spectrum, coulomb, tables)
    solved = exchange_slabs(solved)
    slab = (2, ROWS, GRID, GRID)
    half = (HALF // 2, 2, GRID, GRID)
    with jax.named_scope("backward_planes"):
        exchange, passed, keep, send = call(
            backward_kernel,
            tuple(
                jax.ShapeDtypeStruct(shape, kind)
                for shape, kind in ((slab, F32), (slab, BF16), (half, F32), (half, BF16))
            ),
            [],
            flops,
            operands=6,
        )(core, solved, orbitals, theirs, own, other, tables)
    own, other, passed = total_terms(keep, send, passed)
    outs = jax.ShapeDtypeStruct((STEPS, ROWS, GRID, GRID), BF16)
    total = call(assemble, outs, [], 1 << 20, operands=2)(core, own, other)
    return exchange + passed.astype(F32), total


def solution(mesh):
    return jax.shard_map(
        shards,
        mesh=mesh,
        in_specs=(P("band", "ga", None, None), P(), P()),
        out_specs=(P("band", "ga", None, None), P(None, "ga", None, None)),
        check_vma=False,
    )
```

```python
import functools
import math

import jax
import jax.numpy as jnp
import numpy as np
from jax import lax
from jax.experimental import pallas as pl
from jax.experimental.pallas import tpu as pltpu
from jax.sharding import PartitionSpec as P

COULOMB = math.pi / 8
GRID = 128
STEPS = 2
FIELDS = 2
ROWS = 16
PLANE = GRID + 4
PAIR = 2 * GRID + 4
CHUNK = FIELDS * ROWS * 2 * ROWS
BF16 = jnp.bfloat16
F32 = jnp.float32

SHIFT = 0


def place(z, xl, core):
    return z % 16 * 4 + xl * 2 + core


def near_z(k, j, core):
    return 4 * k + (j + core) % 4 + SHIFT * core


NEAR = [
    [place(near_z(k, j, core), xl, core) for j in range(4) for xl in range(2)]
    for core in range(2)
    for k in range(4)
]
FAR = [
    [place(4 * quarter + z, xl, core) for quarter in (0, 1, 3, 2)]
    for core in range(2)
    for z in range(4)
    for xl in range(2)
]
LINE = [group[xl::2] for group in NEAR for xl in range(2)]
VMEM = pl.BlockSpec(memory_space=pltpu.VMEM)
SMEM = pl.BlockSpec(memory_space=pltpu.SMEM)
HALF = ROWS // 2


def dft_tables():
    indices = np.arange(GRID)
    angles = (indices[:, None] * indices[None, :] % GRID) * (2.0 * np.pi / GRID)
    cosine, sine = np.cos(angles), np.sin(angles)
    matrix = np.block([[cosine, -sine], [sine, cosine]]).astype(np.float32)
    high = matrix.astype(BF16)
    low = (matrix - high.astype(np.float32)).astype(BF16)
    return np.stack([high, low, high.T, low.T])


def dot(a, b):
    return jnp.dot(a, b, preferred_element_type=F32)


def split(x):
    high = x.astype(BF16)
    return high, (x - high.astype(F32)).astype(BF16)


def right(x, tables, which):
    high, low = split(x)
    return dot(high, tables[which]) + (dot(low, tables[which]) + dot(high, tables[which + 1]))


def right_exact(x, tables, which):
    return dot(x, tables[which]) + dot(x, tables[which + 1])


def left(x, tables, which):
    high, low = split(x)
    return dot(tables[which], high) + (dot(tables[which], low) + dot(tables[which + 1], high))


def left_exact(x, tables, which):
    return dot(tables[which], x) + dot(tables[which + 1], x)


def quarter_swap(x):
    n = GRID
    return jnp.concatenate(
        [
            jnp.concatenate([x[:n, :n], x[n:, :n]], axis=1),
            jnp.concatenate([x[:n, n:], x[n:, n:]], axis=1),
        ],
        axis=0,
    )


def halves(core, own, other):
    first = core[0] * HALF
    return [(own, first), (other, HALF - first)]


def forward_kernel(core, ours, theirs, own, other, tables, out, scratch):
    n = GRID
    for f, values in enumerate((ours, theirs)):
        for owner, first in halves(core, own, other):
            for p in range(HALF // 2):
                field = owner[p].reshape(2 * n, n).astype(F32)
                pair = pl.ds(first + 2 * p, 2)
                bands = [values[band, pair].reshape(2 * n, n).astype(F32) for band in range(2)]
                density = jnp.concatenate([band * field for band in bands], axis=1)
                along_z = quarter_swap(right(density, tables, 0))
                along_y = left(along_z, tables, 2)
                start = pl.multiple_of((first + 2 * p) * PLANE, 8)
                for part in range(2):
                    rows = along_y[part * n : (part + 1) * n]
                    scratch[2 * f + part, pl.ds(start, n), :] = rows[:, :n]
                    scratch[2 * f + part, pl.ds(start + PLANE, n), :] = rows[:, n:]

    lane = lax.broadcasted_iota(jnp.int32, (ROWS, n), 1)

    def send(j, carry):
        rest = jnp.zeros((ROWS, n), F32)
        for f in range(FIELDS):
            for k in range(ROWS):
                for part in range(2):
                    field = 2 * f + part
                    tile = scratch[field, pl.ds(j * ROWS + k, ROWS, stride=PLANE), :]
                    high = tile.astype(BF16)
                    row = ((f * ROWS + k) * 2 + part) * ROWS
                    out[j, row : row + ROWS] = high
                    if k == 0:
                        low = tile - high.astype(F32)
                        below = low - low.astype(BF16).astype(F32)
                        rest = jnp.where(lane == field, low[:, :1], rest)
                        rest = jnp.where(lane == field + 2 * FIELDS, below[:, :1], rest)
        out[j, CHUNK:] = rest.astype(BF16)
        return carry

    lax.fori_loop(0, n // ROWS, send, 0)


def solve_kernel(spectrum, coulomb, tables, out, scratch):
    n = GRID
    rest = spectrum[:, CHUNK:].reshape(n, n).astype(F32)
    lane = lax.broadcasted_iota(jnp.int32, (n, n), 1)
    dropped = coulomb[0, :1, :1] == 0.0
    for f in range(FIELDS):

        def pick(k):
            row = (f * ROWS + k) * 2 * ROWS
            ends = [row + part * ROWS for part in range(2)]
            return [spectrum[:, end : end + ROWS].reshape(n, n) for end in ends]

        def factor(q):
            pair = jnp.concatenate([coulomb[2 * q], coulomb[2 * q + 1]], axis=1)
            return jnp.concatenate([pair, pair], axis=0)

        def inverse(x):
            return left_exact(x.astype(BF16), tables, 0)

        def keep(q, solved):
            start = q * 2 * PAIR
            scratch[start : start + 2 * n] = solved[:, :n]
            scratch[start + PAIR : start + PAIR + 2 * n] = solved[:, n:]

        def columns(q):
            both = jnp.concatenate(
                [jnp.concatenate(pick(2 * q), axis=0), jnp.concatenate(pick(2 * q + 1), axis=0)],
                axis=1,
            )
            keep(q, inverse(left_exact(both, tables, 2) * factor(q)))

        parts = []
        for part, tile in enumerate(pick(0)):
            tile, field = tile.astype(F32), 2 * f + part
            low = rest[:, field : field + 1] + rest[:, field + 2 * FIELDS : field + 2 * FIELDS + 1]
            column = tile[:, :1] + low
            mean = jnp.sum(column, axis=0, keepdims=True) * (1.0 / n)
            column = column - jnp.where(dropped, mean, 0.0)
            parts.append(jnp.where(lane == 0, column, tile))
        both = jnp.concatenate(
            [jnp.concatenate(parts, axis=0), jnp.concatenate(pick(1), axis=0).astype(F32)], axis=1
        )
        keep(0, inverse(left(both, tables, 2) * factor(0)))
        for q in range(1, ROWS // 2):
            columns(q)

        def send(i, carry):
            for x in range(ROWS):
                for part in range(2):
                    tile = scratch[pl.ds(part * n + i * ROWS + x, ROWS, stride=PAIR), :]
                    out[i, f, x, part] = tile.astype(BF16)
            return carry

        lax.fori_loop(0, n // ROWS, send, 0)


def backward_kernel(core, solved, ours, theirs, own, other, tables, exchange, passed, keep, send):
    n = GRID
    for (owner, first), terms in zip(halves(core, own, other), (keep, send)):
        for p in range(HALF // 2):
            pair = pl.ds(first + 2 * p, 2)
            field = owner[p].reshape(2 * n, n).astype(F32)
            term = 0.0
            for f, (values, shares) in enumerate(((ours, exchange), (theirs, passed))):

                def pick(x):
                    parts = [solved[:, f, x, part].reshape(n, n) for part in range(2)]
                    return jnp.concatenate(parts, axis=0)

                both = jnp.concatenate([pick(first + 2 * p), pick(first + 2 * p + 1)], axis=1)
                along_y = quarter_swap(left_exact(both, tables, 0))
                potential = right_exact(along_y.astype(BF16), tables, 2)
                for band in range(2):
                    part = potential[:, band * n : (band + 1) * n]
                    share = (part * field).astype(shares.dtype)
                    shares[band, pair] = share.reshape(2, n, n)
                    term = term + part * values[band, pair].reshape(2 * n, n).astype(F32)
            terms[p] = term.astype(terms.dtype).reshape(2, n, n)


def pick_slot(owners, core, step, carry, first_row, orbitals, keep, send):
    first = core[0] * HALF
    for s in range(STEPS):
        slot = lax.rem(owners[s], 2)
        keep[s] = orbitals[slot, pl.ds(first, HALF)]
        send[s] = orbitals[slot, pl.ds(HALF - first, HALF)]


def pick_core(owners, core, kept, received, out):
    for s in range(STEPS):
        ours = lax.rem(lax.div(owners[s], 2), 2) == core[0]

        @pl.when(ours)
        def _():
            for x in range(HALF // 2):
                out[2 * x + s] = kept[s, 2 * x : 2 * x + 2]

        @pl.when(jnp.logical_not(ours))
        def _():
            for x in range(HALF // 2):
                out[2 * x + s] = received[s, 2 * x : 2 * x + 2]


def root_z(owner, core):
    return lax.rem(lax.div(owner, 8) + 16 - SHIFT * core, 16)


def pick_near(owners, core, step, pieces, out):
    owner = owners[step[0]]
    z, xl = root_z(owner, core[0]), lax.rem(lax.div(owner, 4), 2)
    piece = pieces[lax.rem(lax.rem(z, 4) + 4 - core[0], 4) * 2 + xl]
    for copy in range(out.shape[0]):
        out[copy] = piece


def pick_far(owners, core, step, carry, pieces, out):
    quarter = lax.rem(lax.div(root_z(owners[step[0]], core[0]), 4) + carry[0], 4)
    piece = pieces[quarter + jnp.where(quarter == 2, 1, 0) - jnp.where(quarter == 3, 1, 0)]
    for copy in range(out.shape[0]):
        out[copy] = piece


def assemble(core, own, other, out):
    for half, first in halves(core, own, other):
        for s in range(STEPS):
            for x in range(HALF // 2):
                out[s, pl.ds(first + 2 * x, 2)] = half[2 * x + s]


def call(kernel, outs, scratch, flops, scalars=1, operands=4):
    return pl.pallas_call(
        kernel,
        out_shape=outs,
        in_specs=[SMEM] * scalars + [VMEM] * operands,
        scratch_shapes=scratch,
        compiler_params=pltpu.CompilerParams(vmem_limit_bytes=20 * 1024 * 1024),
        cost_estimate=pl.CostEstimate(flops=flops, bytes_accessed=5 << 20, transcendentals=0),
    )


def exchange_all(x, groups):
    return lax.all_to_all(x, "band", 0, 0, axis_index_groups=groups, tiled=True)


def gather_all(x, groups):
    return exchange_all(jnp.broadcast_to(x[None], (len(groups[0]),) + x.shape), groups)


def exchange_slabs(x):
    return lax.all_to_all(x, "ga", 0, 0, tiled=True)


def swap(x, bit):
    return lax.ppermute(x, "band", [(i, i ^ bit) for i in range(64)])


def pick(kernel, shape, scalars, *pieces):
    outs = jax.ShapeDtypeStruct(shape + (GRID, GRID), BF16)
    return call(kernel, outs, [], 1 << 20, scalars=len(scalars), operands=len(pieces))(*scalars, *pieces)


def spread_owners(orbitals, owners, core, step, carry, first_row):
    half = jax.ShapeDtypeStruct((STEPS, HALF, GRID, GRID), BF16)
    scalars = (owners, core, step, carry, first_row.reshape(1))
    keep, send = call(pick_slot, (half, half), [], 1 << 20, scalars=5, operands=1)(*scalars, orbitals)
    received = swap(send, 1)
    piece = exchange_all(pick(pick_core, (8, 2), (owners, core), keep, received), NEAR)
    orbitals, piece = lax.optimization_barrier((orbitals, piece))
    theirs = swap(orbitals, 2)
    piece = exchange_all(pick(pick_near, (4, 2), (owners, core, step), piece), FAR)
    theirs, piece = lax.optimization_barrier((theirs, piece))
    piece = exchange_all(pick(pick_far, (4, 2), (owners, core, step, carry), piece), LINE)
    return theirs, piece


def total_terms(keep, send, passed):
    piece = (keep + swap(send, 1).astype(F32)).astype(BF16)
    piece = jnp.sum(exchange_all(piece, LINE).astype(F32), axis=0).astype(BF16)
    passed, piece = lax.optimization_barrier((passed, piece))
    passed = swap(passed, 2)
    piece = jnp.sum(gather_all(piece, FAR).astype(F32), axis=0).astype(BF16)
    passed, piece = lax.optimization_barrier((passed, piece))
    own = gather_all(piece, NEAR)
    return own, swap(own, 1), passed


def coulomb_slab(cutoff, first_row):
    mirrored = jnp.roll(cutoff[::-1, ::-1], (1, 1), (0, 1))
    limits = lax.dynamic_slice_in_dim(jnp.minimum(cutoff, mirrored), first_row, ROWS, 1).T
    signed = np.arange(GRID, dtype=np.int32)
    signed = np.where(signed < GRID // 2, signed, signed - GRID).astype(np.int32)
    own = first_row + np.arange(ROWS, dtype=np.int32)
    own = jnp.where(own < GRID // 2, own, own - GRID)
    squared = own[:, None, None] ** 2 + signed[None, :, None] ** 2 + signed[None, None, :] ** 2
    inside = (np.abs(signed)[None, None, :] <= limits[:, :, None]) & (squared > 0)
    scale = COULOMB * float(GRID) ** 1.5 / float(GRID) ** 3
    return jnp.where(inside, scale / jnp.maximum(squared, 1).astype(F32), 0.0)


def shards(orbitals, owners, cutoff):
    first_row = (lax.axis_index("ga") * ROWS).astype(jnp.int32)
    tables = jnp.asarray(dft_tables())
    band = lax.axis_index("band")
    core = (band % 2).astype(jnp.int32).reshape(1)
    step = (band // 2 % 2).astype(jnp.int32).reshape(1)
    carry = jnp.where((band % 2 == 1) & (band // 4 % 4 < SHIFT), 1, 0).astype(jnp.int32).reshape(1)
    theirs, own = spread_owners(orbitals, owners, core, step, carry, first_row)
    cutoff, first_row, own = lax.optimization_barrier((cutoff, first_row, own))
    other = swap(own, 1)
    coulomb, other = lax.optimization_barrier((coulomb_slab(cutoff, first_row), other))
    flops = 2 * 2 * FIELDS * 3 * 8 * 256**3
    with jax.named_scope("forward_planes"):
        spectrum = call(
            forward_kernel,
            jax.ShapeDtypeStruct((8, CHUNK + ROWS, GRID), BF16),
            [pltpu.VMEM((2 * FIELDS, ROWS * PLANE, GRID), F32)],
            flops,
            operands=5,
        )(core, orbitals, theirs, own, other, tables)
    spectrum = exchange_slabs(spectrum)
    with jax.named_scope("coulomb_solve"):
        solved = call(
            solve_kernel,
            jax.ShapeDtypeStruct((8, FIELDS, ROWS, 2, ROWS, GRID), BF16),
            [pltpu.VMEM((ROWS * PAIR, GRID), F32)],
            flops,
            scalars=0,
            operands=3,
        )(spectrum, coulomb, tables)
    solved = exchange_slabs(solved)
    slab = (2, ROWS, GRID, GRID)
    half = (HALF // 2, 2, GRID, GRID)
    with jax.named_scope("backward_planes"):
        exchange, passed, keep, send = call(
            backward_kernel,
            tuple(
                jax.ShapeDtypeStruct(shape, kind)
                for shape, kind in ((slab, F32), (slab, BF16), (half, F32), (half, BF16))
            ),
            [],
            flops,
            operands=6,
        )(core, solved, orbitals, theirs, own, other, tables)
    own, other, passed = total_terms(keep, send, passed)
    outs = jax.ShapeDtypeStruct((STEPS, ROWS, GRID, GRID), BF16)
    total = call(assemble, outs, [], 1 << 20, operands=2)(core, own, other)
    return exchange + passed.astype(F32), total


def solution(mesh):
    return jax.shard_map(
        shards,
        mesh=mesh,
        in_specs=(P("band", "ga", None, None), P(), P()),
        out_specs=(P("band", "ga", None, None), P(None, "ga", None, None)),
        check_vma=False,
    )
```

```python
import functools
import math

import jax
import jax.numpy as jnp
import numpy as np
from jax import lax
from jax.experimental import pallas as pl
from jax.experimental.pallas import tpu as pltpu
from jax.sharding import PartitionSpec as P

COULOMB = math.pi / 8
GRID = 128
STEPS = 2
FIELDS = 2
ROWS = 16
PLANE = GRID + 4
PAIR = 2 * GRID + 4
CHUNK = FIELDS * ROWS * 2 * ROWS
BF16 = jnp.bfloat16
F32 = jnp.float32

SHIFT = 0


def place(z, xl, core):
    return z % 16 * 4 + xl * 2 + core


def near_z(k, j, core):
    return 4 * k + (j + core) % 4 + SHIFT * core


NEAR = [
    [place(near_z(k, j, core), xl, core) for j in range(4) for xl in range(2)]
    for core in range(2)
    for k in range(4)
]
FAR = [
    [place(4 * quarter + z, xl, core) for quarter in (0, 1, 3, 2)]
    for core in range(2)
    for z in range(4)
    for xl in range(2)
]
SLABS = [[band * 8 + (7 - g if band % 2 else g) for g in range(8)] for band in range(64)]
LINE = [group[xl::2] for group in NEAR for xl in range(2)]
VMEM = pl.BlockSpec(memory_space=pltpu.VMEM)
SMEM = pl.BlockSpec(memory_space=pltpu.SMEM)
HALF = ROWS // 2


def dft_tables():
    indices = np.arange(GRID)
    angles = (indices[:, None] * indices[None, :] % GRID) * (2.0 * np.pi / GRID)
    cosine, sine = np.cos(angles), np.sin(angles)
    matrix = np.block([[cosine, -sine], [sine, cosine]]).astype(np.float32)
    high = matrix.astype(BF16)
    low = (matrix - high.astype(np.float32)).astype(BF16)
    plain = np.stack([high, low, high.T, low.T])
    order = np.arange(2 * GRID).reshape(2, GRID // ROWS, ROWS)[:, ::-1].reshape(-1)
    turned = np.stack([high[order], low[order], high.T[:, order], low.T[:, order]])
    return plain, np.concatenate([plain, turned])


def dot(a, b):
    return jnp.dot(a, b, preferred_element_type=F32)


def split(x):
    high = x.astype(BF16)
    return high, (x - high.astype(F32)).astype(BF16)


def right(x, tables, which):
    high, low = split(x)
    return dot(high, tables[which]) + (dot(low, tables[which]) + dot(high, tables[which + 1]))


def right_exact(x, tables, which):
    return dot(x, tables[which]) + dot(x, tables[which + 1])


def left(x, tables, which):
    high, low = split(x)
    return dot(tables[which], high) + (dot(tables[which], low) + dot(tables[which + 1], high))


def left_exact(x, tables, which):
    return dot(tables[which], x) + dot(tables[which + 1], x)


def quarter_swap(x):
    n = GRID
    return jnp.concatenate(
        [
            jnp.concatenate([x[:n, :n], x[n:, :n]], axis=1),
            jnp.concatenate([x[:n, n:], x[n:, n:]], axis=1),
        ],
        axis=0,
    )


def halves(core, own, other):
    first = core[0] * HALF
    return [(own, first), (other, HALF - first)]


def forward_kernel(core, ours, theirs, own, other, tables, out, scratch):
    n = GRID
    for f, values in enumerate((ours, theirs)):
        for owner, first in halves(core, own, other):
            for p in range(HALF // 2):
                field = owner[p].reshape(2 * n, n).astype(F32)
                pair = pl.ds(first + 2 * p, 2)
                bands = [values[band, pair].reshape(2 * n, n).astype(F32) for band in range(2)]
                density = jnp.concatenate([band * field for band in bands], axis=1)
                along_z = quarter_swap(right(density, tables, 0))
                along_y = left(along_z, tables, 2)
                start = pl.multiple_of((first + 2 * p) * PLANE, 8)
                for part in range(2):
                    rows = along_y[part * n : (part + 1) * n]
                    scratch[2 * f + part, pl.ds(start, n), :] = rows[:, :n]
                    scratch[2 * f + part, pl.ds(start + PLANE, n), :] = rows[:, n:]

    lane = lax.broadcasted_iota(jnp.int32, (ROWS, n), 1)

    def send(j, carry):
        rest = jnp.zeros((ROWS, n), F32)
        for f in range(FIELDS):
            for k in range(ROWS):
                for part in range(2):
                    field = 2 * f + part
                    tile = scratch[field, pl.ds(j * ROWS + k, ROWS, stride=PLANE), :]
                    high = tile.astype(BF16)
                    row = ((f * ROWS + k) * 2 + part) * ROWS
                    out[j, row : row + ROWS] = high
                    if k == 0:
                        low = tile - high.astype(F32)
                        below = low - low.astype(BF16).astype(F32)
                        rest = jnp.where(lane == field, low[:, :1], rest)
                        rest = jnp.where(lane == field + 2 * FIELDS, below[:, :1], rest)
        out[j, CHUNK:] = rest.astype(BF16)
        return carry

    lax.fori_loop(0, n // ROWS, send, 0)


def solve_kernel(core, spectrum, coulomb, tables, out, scratch):
    n = GRID
    first = core[0] * 4
    rest = spectrum[:, CHUNK:].reshape(n, n).astype(F32)
    lane = lax.broadcasted_iota(jnp.int32, (n, n), 1)
    dropped = coulomb[0, :1, :1] == 0.0
    for f in range(FIELDS):

        def pick(k):
            row = (f * ROWS + k) * 2 * ROWS
            ends = [row + part * ROWS for part in range(2)]
            return [spectrum[:, end : end + ROWS].reshape(n, n) for end in ends]

        def factor(q):
            pair = jnp.concatenate([coulomb[2 * q], coulomb[2 * q + 1]], axis=1)
            return jnp.concatenate([pair, pair], axis=0)

        def inverse(x):
            return left_exact(x.astype(BF16), tables, first)

        def keep(q, solved):
            start = q * 2 * PAIR
            scratch[start : start + 2 * n] = solved[:, :n]
            scratch[start + PAIR : start + PAIR + 2 * n] = solved[:, n:]

        def columns(q):
            both = jnp.concatenate(
                [jnp.concatenate(pick(2 * q), axis=0), jnp.concatenate(pick(2 * q + 1), axis=0)],
                axis=1,
            )
            keep(q, inverse(left_exact(both, tables, first + 2) * factor(q)))

        parts = []
        for part, tile in enumerate(pick(0)):
            tile, field = tile.astype(F32), 2 * f + part
            low = rest[:, field : field + 1] + rest[:, field + 2 * FIELDS : field + 2 * FIELDS + 1]
            column = tile[:, :1] + low
            mean = jnp.sum(column, axis=0, keepdims=True) * (1.0 / n)
            column = column - jnp.where(dropped, mean, 0.0)
            parts.append(jnp.where(lane == 0, column, tile))
        both = jnp.concatenate(
            [jnp.concatenate(parts, axis=0), jnp.concatenate(pick(1), axis=0).astype(F32)], axis=1
        )
        keep(0, inverse(left(both, tables, first + 2) * factor(0)))
        for q in range(1, ROWS // 2):
            columns(q)

        def send(i, carry):
            for x in range(ROWS):
                for part in range(2):
                    tile = scratch[pl.ds(part * n + i * ROWS + x, ROWS, stride=PAIR), :]
                    out[i, f, x, part] = tile.astype(BF16)
            return carry

        lax.fori_loop(0, n // ROWS, send, 0)


def backward_kernel(core, solved, ours, theirs, own, other, tables, exchange, passed, keep, send):
    n = GRID
    for (owner, first), terms in zip(halves(core, own, other), (keep, send)):
        for p in range(HALF // 2):
            pair = pl.ds(first + 2 * p, 2)
            field = owner[p].reshape(2 * n, n).astype(F32)
            term = 0.0
            for f, (values, shares) in enumerate(((ours, exchange), (theirs, passed))):

                def pick(x):
                    parts = [solved[:, f, x, part].reshape(n, n) for part in range(2)]
                    return jnp.concatenate(parts, axis=0)

                both = jnp.concatenate([pick(first + 2 * p), pick(first + 2 * p + 1)], axis=1)
                along_y = quarter_swap(left_exact(both, tables, 0))
                potential = right_exact(along_y.astype(BF16), tables, 2)
                for band in range(2):
                    part = potential[:, band * n : (band + 1) * n]
                    share = (part * field).astype(shares.dtype)
                    shares[band, pair] = share.reshape(2, n, n)
                    term = term + part * values[band, pair].reshape(2 * n, n).astype(F32)
            terms[p] = term.astype(terms.dtype).reshape(2, n, n)


def pick_slot(owners, core, step, carry, first_row, orbitals, keep, send):
    first = core[0] * HALF
    for s in range(STEPS):
        slot = lax.rem(owners[s], 2)
        keep[s] = orbitals[slot, pl.ds(first, HALF)]
        send[s] = orbitals[slot, pl.ds(HALF - first, HALF)]


def pick_core(owners, core, kept, received, out):
    for s in range(STEPS):
        ours = lax.rem(lax.div(owners[s], 2), 2) == core[0]

        @pl.when(ours)
        def _():
            for x in range(HALF // 2):
                out[2 * x + s] = kept[s, 2 * x : 2 * x + 2]

        @pl.when(jnp.logical_not(ours))
        def _():
            for x in range(HALF // 2):
                out[2 * x + s] = received[s, 2 * x : 2 * x + 2]


def root_z(owner, core):
    return lax.rem(lax.div(owner, 8) + 16 - SHIFT * core, 16)


def pick_near(owners, core, step, pieces, out):
    owner = owners[step[0]]
    z, xl = root_z(owner, core[0]), lax.rem(lax.div(owner, 4), 2)
    piece = pieces[lax.rem(lax.rem(z, 4) + 4 - core[0], 4) * 2 + xl]
    for copy in range(out.shape[0]):
        out[copy] = piece


def pick_far(owners, core, step, carry, pieces, out):
    quarter = lax.rem(lax.div(root_z(owners[step[0]], core[0]), 4) + carry[0], 4)
    piece = pieces[quarter + jnp.where(quarter == 2, 1, 0) - jnp.where(quarter == 3, 1, 0)]
    for copy in range(out.shape[0]):
        out[copy] = piece


def assemble(core, own, other, out):
    for half, first in halves(core, own, other):
        for s in range(STEPS):
            for x in range(HALF // 2):
                out[s, pl.ds(first + 2 * x, 2)] = half[2 * x + s]


def call(kernel, outs, scratch, flops, scalars=1, operands=4):
    return pl.pallas_call(
        kernel,
        out_shape=outs,
        in_specs=[SMEM] * scalars + [VMEM] * operands,
        scratch_shapes=scratch,
        compiler_params=pltpu.CompilerParams(vmem_limit_bytes=20 * 1024 * 1024),
        cost_estimate=pl.CostEstimate(flops=flops, bytes_accessed=5 << 20, transcendentals=0),
    )


def exchange_all(x, groups):
    return lax.all_to_all(x, "band", 0, 0, axis_index_groups=groups, tiled=True)


def gather_all(x, groups):
    return exchange_all(jnp.broadcast_to(x[None], (len(groups[0]),) + x.shape), groups)


def exchange_slabs(x):
    return lax.all_to_all(x, ("band", "ga"), 0, 0, axis_index_groups=SLABS, tiled=True)


def swap(x, bit):
    return lax.ppermute(x, "band", [(i, i ^ bit) for i in range(64)])


def pick(kernel, shape, scalars, *pieces):
    outs = jax.ShapeDtypeStruct(shape + (GRID, GRID), BF16)
    return call(kernel, outs, [], 1 << 20, scalars=len(scalars), operands=len(pieces))(*scalars, *pieces)


def spread_owners(orbitals, owners, core, step, carry, first_row):
    half = jax.ShapeDtypeStruct((STEPS, HALF, GRID, GRID), BF16)
    scalars = (owners, core, step, carry, first_row.reshape(1))
    keep, send = call(pick_slot, (half, half), [], 1 << 20, scalars=5, operands=1)(*scalars, orbitals)
    received = swap(send, 1)
    piece = exchange_all(pick(pick_core, (8, 2), (owners, core), keep, received), NEAR)
    orbitals, piece = lax.optimization_barrier((orbitals, piece))
    theirs = swap(orbitals, 2)
    piece = exchange_all(pick(pick_near, (4, 2), (owners, core, step), piece), FAR)
    theirs, piece = lax.optimization_barrier((theirs, piece))
    piece = exchange_all(pick(pick_far, (4, 2), (owners, core, step, carry), piece), LINE)
    return theirs, piece


def total_terms(keep, send, passed):
    piece = (keep + swap(send, 1).astype(F32)).astype(BF16)
    piece = jnp.sum(exchange_all(piece, LINE).astype(F32), axis=0).astype(BF16)
    passed, piece = lax.optimization_barrier((passed, piece))
    passed = swap(passed, 2)
    piece = jnp.sum(gather_all(piece, FAR).astype(F32), axis=0).astype(BF16)
    passed, piece = lax.optimization_barrier((passed, piece))
    own = gather_all(piece, NEAR)
    return own, swap(own, 1), passed


def coulomb_slab(cutoff, first_row):
    mirrored = jnp.roll(cutoff[::-1, ::-1], (1, 1), (0, 1))
    limits = lax.dynamic_slice_in_dim(jnp.minimum(cutoff, mirrored), first_row, ROWS, 1).T
    signed = np.arange(GRID, dtype=np.int32)
    signed = np.where(signed < GRID // 2, signed, signed - GRID).astype(np.int32)
    own = first_row + np.arange(ROWS, dtype=np.int32)
    own = jnp.where(own < GRID // 2, own, own - GRID)
    squared = own[:, None, None] ** 2 + signed[None, :, None] ** 2 + signed[None, None, :] ** 2
    inside = (np.abs(signed)[None, None, :] <= limits[:, :, None]) & (squared > 0)
    scale = COULOMB * float(GRID) ** 1.5 / float(GRID) ** 3
    return jnp.where(inside, scale / jnp.maximum(squared, 1).astype(F32), 0.0)


def shards(orbitals, owners, cutoff):
    slab = lax.axis_index("ga")
    first_row = (jnp.where(lax.axis_index("band") % 2 == 1, 7 - slab, slab) * ROWS).astype(jnp.int32)
    tables, both_tables = (jnp.asarray(table) for table in dft_tables())
    band = lax.axis_index("band")
    core = (band % 2).astype(jnp.int32).reshape(1)
    step = (band // 2 % 2).astype(jnp.int32).reshape(1)
    carry = jnp.where((band % 2 == 1) & (band // 4 % 4 < SHIFT), 1, 0).astype(jnp.int32).reshape(1)
    theirs, own = spread_owners(orbitals, owners, core, step, carry, first_row)
    cutoff, first_row, own = lax.optimization_barrier((cutoff, first_row, own))
    other = swap(own, 1)
    coulomb, other = lax.optimization_barrier((coulomb_slab(cutoff, first_row), other))
    flops = 2 * 2 * FIELDS * 3 * 8 * 256**3
    with jax.named_scope("forward_planes"):
        spectrum = call(
            forward_kernel,
            jax.ShapeDtypeStruct((8, CHUNK + ROWS, GRID), BF16),
            [pltpu.VMEM((2 * FIELDS, ROWS * PLANE, GRID), F32)],
            flops,
            operands=5,
        )(core, orbitals, theirs, own, other, tables)
    spectrum = exchange_slabs(spectrum)
    with jax.named_scope("coulomb_solve"):
        solved = call(
            solve_kernel,
            jax.ShapeDtypeStruct((8, FIELDS, ROWS, 2, ROWS, GRID), BF16),
            [pltpu.VMEM((ROWS * PAIR, GRID), F32)],
            flops,
            operands=3,
        )(core, spectrum, coulomb, both_tables)
    solved = exchange_slabs(solved)
    slab = (2, ROWS, GRID, GRID)
    half = (HALF // 2, 2, GRID, GRID)
    with jax.named_scope("backward_planes"):
        exchange, passed, keep, send = call(
            backward_kernel,
            tuple(
                jax.ShapeDtypeStruct(shape, kind)
                for shape, kind in ((slab, F32), (slab, BF16), (half, F32), (half, BF16))
            ),
            [],
            flops,
            operands=6,
        )(core, solved, orbitals, theirs, own, other, tables)
    own, other, passed = total_terms(keep, send, passed)
    outs = jax.ShapeDtypeStruct((STEPS, ROWS, GRID, GRID), BF16)
    total = call(assemble, outs, [], 1 << 20, operands=2)(core, own, other)
    return exchange + passed.astype(F32), total


def solution(mesh):
    return jax.shard_map(
        shards,
        mesh=mesh,
        in_specs=(P("band", "ga", None, None), P(), P()),
        out_specs=(P("band", "ga", None, None), P(None, "ga", None, None)),
        check_vma=False,
    )
```

```python
import functools
import math

import jax
import jax.numpy as jnp
import numpy as np
from jax import lax
from jax.experimental import pallas as pl
from jax.experimental.pallas import tpu as pltpu
from jax.sharding import PartitionSpec as P

COULOMB = math.pi / 8
GRID = 128
STEPS = 2
FIELDS = 2
ROWS = 16
PLANE = GRID + 4
PAIR = 2 * GRID + 4
CHUNK = FIELDS * ROWS * 2 * ROWS
BF16 = jnp.bfloat16
F32 = jnp.float32

SHIFT = 0


def place(z, xl, core):
    return z % 16 * 4 + xl * 2 + core


def near_z(k, j, core):
    return 4 * k + (j + core) % 4 + SHIFT * core


NEAR = [
    [place(near_z(k, j, core), xl, core) for j in range(4) for xl in range(2)]
    for core in range(2)
    for k in range(4)
]
FAR = [
    [place(4 * quarter + z, xl, core) for quarter in (0, 1, 3, 2)]
    for core in range(2)
    for z in range(4)
    for xl in range(2)
]
MASKS = (0, 7, 4, 3)
SLABS = [[band * 8 + (g ^ MASKS[band % 4]) for g in range(8)] for band in range(64)]
LINE = [group[xl::2] for group in NEAR for xl in range(2)]
VMEM = pl.BlockSpec(memory_space=pltpu.VMEM)
SMEM = pl.BlockSpec(memory_space=pltpu.SMEM)
HALF = ROWS // 2


def dft_tables():
    indices = np.arange(GRID)
    angles = (indices[:, None] * indices[None, :] % GRID) * (2.0 * np.pi / GRID)
    cosine, sine = np.cos(angles), np.sin(angles)
    matrix = np.block([[cosine, -sine], [sine, cosine]]).astype(np.float32)
    high = matrix.astype(BF16)
    low = (matrix - high.astype(np.float32)).astype(BF16)
    plain = np.stack([high, low, high.T, low.T])
    kinds = []
    for mask in MASKS:
        order = np.arange(2 * GRID).reshape(2, 8, ROWS)[:, np.arange(8) ^ mask].reshape(-1)
        kinds += [high[order], low[order], high.T[:, order], low.T[:, order]]
    return plain, np.stack(kinds)


def dot(a, b):
    return jnp.dot(a, b, preferred_element_type=F32)


def split(x):
    high = x.astype(BF16)
    return high, (x - high.astype(F32)).astype(BF16)


def right(x, tables, which):
    high, low = split(x)
    return dot(high, tables[which]) + (dot(low, tables[which]) + dot(high, tables[which + 1]))


def right_exact(x, tables, which):
    return dot(x, tables[which]) + dot(x, tables[which + 1])


def left(x, tables, which):
    high, low = split(x)
    return dot(tables[which], high) + (dot(tables[which], low) + dot(tables[which + 1], high))


def left_exact(x, tables, which):
    return dot(tables[which], x) + dot(tables[which + 1], x)


def quarter_swap(x):
    n = GRID
    return jnp.concatenate(
        [
            jnp.concatenate([x[:n, :n], x[n:, :n]], axis=1),
            jnp.concatenate([x[:n, n:], x[n:, n:]], axis=1),
        ],
        axis=0,
    )


def halves(core, own, other):
    first = core[0] * HALF
    return [(own, first), (other, HALF - first)]


def forward_kernel(core, ours, theirs, own, other, tables, out, scratch):
    n = GRID
    for f, values in enumerate((ours, theirs)):
        for owner, first in halves(core, own, other):
            for p in range(HALF // 2):
                field = owner[p].reshape(2 * n, n).astype(F32)
                pair = pl.ds(first + 2 * p, 2)
                bands = [values[band, pair].reshape(2 * n, n).astype(F32) for band in range(2)]
                density = jnp.concatenate([band * field for band in bands], axis=1)
                along_z = quarter_swap(right(density, tables, 0))
                along_y = left(along_z, tables, 2)
                start = pl.multiple_of((first + 2 * p) * PLANE, 8)
                for part in range(2):
                    rows = along_y[part * n : (part + 1) * n]
                    scratch[2 * f + part, pl.ds(start, n), :] = rows[:, :n]
                    scratch[2 * f + part, pl.ds(start + PLANE, n), :] = rows[:, n:]

    lane = lax.broadcasted_iota(jnp.int32, (ROWS, n), 1)

    def send(j, carry):
        rest = jnp.zeros((ROWS, n), F32)
        for f in range(FIELDS):
            for k in range(ROWS):
                for part in range(2):
                    field = 2 * f + part
                    tile = scratch[field, pl.ds(j * ROWS + k, ROWS, stride=PLANE), :]
                    high = tile.astype(BF16)
                    row = ((f * ROWS + k) * 2 + part) * ROWS
                    out[j, row : row + ROWS] = high
                    if k == 0:
                        low = tile - high.astype(F32)
                        below = low - low.astype(BF16).astype(F32)
                        rest = jnp.where(lane == field, low[:, :1], rest)
                        rest = jnp.where(lane == field + 2 * FIELDS, below[:, :1], rest)
        out[j, CHUNK:] = rest.astype(BF16)
        return carry

    lax.fori_loop(0, n // ROWS, send, 0)


def solve_kernel(kind, spectrum, coulomb, tables, out, scratch):
    n = GRID
    first = kind[0] * 4
    rest = spectrum[:, CHUNK:].reshape(n, n).astype(F32)
    lane = lax.broadcasted_iota(jnp.int32, (n, n), 1)
    dropped = coulomb[0, :1, :1] == 0.0
    for f in range(FIELDS):

        def pick(k):
            row = (f * ROWS + k) * 2 * ROWS
            ends = [row + part * ROWS for part in range(2)]
            return [spectrum[:, end : end + ROWS].reshape(n, n) for end in ends]

        def factor(q):
            pair = jnp.concatenate([coulomb[2 * q], coulomb[2 * q + 1]], axis=1)
            return jnp.concatenate([pair, pair], axis=0)

        def inverse(x):
            return left_exact(x.astype(BF16), tables, first)

        def keep(q, solved):
            start = q * 2 * PAIR
            scratch[start : start + 2 * n] = solved[:, :n]
            scratch[start + PAIR : start + PAIR + 2 * n] = solved[:, n:]

        def columns(q):
            both = jnp.concatenate(
                [jnp.concatenate(pick(2 * q), axis=0), jnp.concatenate(pick(2 * q + 1), axis=0)],
                axis=1,
            )
            keep(q, inverse(left_exact(both, tables, first + 2) * factor(q)))

        parts = []
        for part, tile in enumerate(pick(0)):
            tile, field = tile.astype(F32), 2 * f + part
            low = rest[:, field : field + 1] + rest[:, field + 2 * FIELDS : field + 2 * FIELDS + 1]
            column = tile[:, :1] + low
            mean = jnp.sum(column, axis=0, keepdims=True) * (1.0 / n)
            column = column - jnp.where(dropped, mean, 0.0)
            parts.append(jnp.where(lane == 0, column, tile))
        both = jnp.concatenate(
            [jnp.concatenate(parts, axis=0), jnp.concatenate(pick(1), axis=0).astype(F32)], axis=1
        )
        keep(0, inverse(left(both, tables, first + 2) * factor(0)))
        for q in range(1, ROWS // 2):
            columns(q)

        def send(i, carry):
            for x in range(ROWS):
                for part in range(2):
                    tile = scratch[pl.ds(part * n + i * ROWS + x, ROWS, stride=PAIR), :]
                    out[i, f, x, part] = tile.astype(BF16)
            return carry

        lax.fori_loop(0, n // ROWS, send, 0)


def backward_kernel(core, solved, ours, theirs, own, other, tables, exchange, passed, keep, send):
    n = GRID
    for (owner, first), terms in zip(halves(core, own, other), (keep, send)):
        for p in range(HALF // 2):
            pair = pl.ds(first + 2 * p, 2)
            field = owner[p].reshape(2 * n, n).astype(F32)
            term = 0.0
            for f, (values, shares) in enumerate(((ours, exchange), (theirs, passed))):

                def pick(x):
                    parts = [solved[:, f, x, part].reshape(n, n) for part in range(2)]
                    return jnp.concatenate(parts, axis=0)

                both = jnp.concatenate([pick(first + 2 * p), pick(first + 2 * p + 1)], axis=1)
                along_y = quarter_swap(left_exact(both, tables, 0))
                potential = right_exact(along_y.astype(BF16), tables, 2)
                for band in range(2):
                    part = potential[:, band * n : (band + 1) * n]
                    share = (part * field).astype(shares.dtype)
                    shares[band, pair] = share.reshape(2, n, n)
                    term = term + part * values[band, pair].reshape(2 * n, n).astype(F32)
            terms[p] = term.astype(terms.dtype).reshape(2, n, n)


def pick_slot(owners, core, step, carry, first_row, orbitals, keep, send):
    first = core[0] * HALF
    for s in range(STEPS):
        slot = lax.rem(owners[s], 2)
        keep[s] = orbitals[slot, pl.ds(first, HALF)]
        send[s] = orbitals[slot, pl.ds(HALF - first, HALF)]


def pick_core(owners, core, kept, received, out):
    for s in range(STEPS):
        ours = lax.rem(lax.div(owners[s], 2), 2) == core[0]

        @pl.when(ours)
        def _():
            for x in range(HALF // 2):
                out[2 * x + s] = kept[s, 2 * x : 2 * x + 2]

        @pl.when(jnp.logical_not(ours))
        def _():
            for x in range(HALF // 2):
                out[2 * x + s] = received[s, 2 * x : 2 * x + 2]


def root_z(owner, core):
    return lax.rem(lax.div(owner, 8) + 16 - SHIFT * core, 16)


def pick_near(owners, core, step, pieces, out):
    owner = owners[step[0]]
    z, xl = root_z(owner, core[0]), lax.rem(lax.div(owner, 4), 2)
    piece = pieces[lax.rem(lax.rem(z, 4) + 4 - core[0], 4) * 2 + xl]
    for copy in range(out.shape[0]):
        out[copy] = piece


def pick_far(owners, core, step, carry, pieces, out):
    quarter = lax.rem(lax.div(root_z(owners[step[0]], core[0]), 4) + carry[0], 4)
    piece = pieces[quarter + jnp.where(quarter == 2, 1, 0) - jnp.where(quarter == 3, 1, 0)]
    for copy in range(out.shape[0]):
        out[copy] = piece


def assemble(core, own, other, out):
    for half, first in halves(core, own, other):
        for s in range(STEPS):
            for x in range(HALF // 2):
                out[s, pl.ds(first + 2 * x, 2)] = half[2 * x + s]


def call(kernel, outs, scratch, flops, scalars=1, operands=4):
    return pl.pallas_call(
        kernel,
        out_shape=outs,
        in_specs=[SMEM] * scalars + [VMEM] * operands,
        scratch_shapes=scratch,
        compiler_params=pltpu.CompilerParams(vmem_limit_bytes=20 * 1024 * 1024),
        cost_estimate=pl.CostEstimate(flops=flops, bytes_accessed=5 << 20, transcendentals=0),
    )


def exchange_all(x, groups):
    return lax.all_to_all(x, "band", 0, 0, axis_index_groups=groups, tiled=True)


def gather_all(x, groups):
    return exchange_all(jnp.broadcast_to(x[None], (len(groups[0]),) + x.shape), groups)


def exchange_slabs(x):
    return lax.all_to_all(x, ("band", "ga"), 0, 0, axis_index_groups=SLABS, tiled=True)


def swap(x, bit):
    return lax.ppermute(x, "band", [(i, i ^ bit) for i in range(64)])


def pick(kernel, shape, scalars, *pieces):
    outs = jax.ShapeDtypeStruct(shape + (GRID, GRID), BF16)
    return call(kernel, outs, [], 1 << 20, scalars=len(scalars), operands=len(pieces))(*scalars, *pieces)


def spread_owners(orbitals, owners, core, step, carry, first_row):
    half = jax.ShapeDtypeStruct((STEPS, HALF, GRID, GRID), BF16)
    scalars = (owners, core, step, carry, first_row.reshape(1))
    keep, send = call(pick_slot, (half, half), [], 1 << 20, scalars=5, operands=1)(*scalars, orbitals)
    received = swap(send, 1)
    piece = exchange_all(pick(pick_core, (8, 2), (owners, core), keep, received), NEAR)
    orbitals, piece = lax.optimization_barrier((orbitals, piece))
    theirs = swap(orbitals, 2)
    piece = exchange_all(pick(pick_near, (4, 2), (owners, core, step), piece), FAR)
    theirs, piece = lax.optimization_barrier((theirs, piece))
    piece = exchange_all(pick(pick_far, (4, 2), (owners, core, step, carry), piece), LINE)
    return theirs, piece


def total_terms(keep, send, passed):
    piece = (keep + swap(send, 1).astype(F32)).astype(BF16)
    piece = jnp.sum(exchange_all(piece, LINE).astype(F32), axis=0).astype(BF16)
    passed, piece = lax.optimization_barrier((passed, piece))
    passed = swap(passed, 2)
    piece = jnp.sum(gather_all(piece, FAR).astype(F32), axis=0).astype(BF16)
    passed, piece = lax.optimization_barrier((passed, piece))
    own = gather_all(piece, NEAR)
    return own, swap(own, 1), passed


def coulomb_slab(cutoff, first_row):
    mirrored = jnp.roll(cutoff[::-1, ::-1], (1, 1), (0, 1))
    limits = lax.dynamic_slice_in_dim(jnp.minimum(cutoff, mirrored), first_row, ROWS, 1).T
    signed = np.arange(GRID, dtype=np.int32)
    signed = np.where(signed < GRID // 2, signed, signed - GRID).astype(np.int32)
    own = first_row + np.arange(ROWS, dtype=np.int32)
    own = jnp.where(own < GRID // 2, own, own - GRID)
    squared = own[:, None, None] ** 2 + signed[None, :, None] ** 2 + signed[None, None, :] ** 2
    inside = (np.abs(signed)[None, None, :] <= limits[:, :, None]) & (squared > 0)
    scale = COULOMB * float(GRID) ** 1.5 / float(GRID) ** 3
    return jnp.where(inside, scale / jnp.maximum(squared, 1).astype(F32), 0.0)


def shards(orbitals, owners, cutoff):
    slab = lax.axis_index("ga")
    kind = lax.axis_index("band") % 4
    mask = jnp.where(kind % 2 == 1, 7, 0) ^ jnp.where(kind >= 2, 4, 0)
    first_row = ((slab ^ mask) * ROWS).astype(jnp.int32)
    tables, both_tables = (jnp.asarray(table) for table in dft_tables())
    band = lax.axis_index("band")
    core = (band % 2).astype(jnp.int32).reshape(1)
    step = (band // 2 % 2).astype(jnp.int32).reshape(1)
    carry = jnp.where((band % 2 == 1) & (band // 4 % 4 < SHIFT), 1, 0).astype(jnp.int32).reshape(1)
    theirs, own = spread_owners(orbitals, owners, core, step, carry, first_row)
    cutoff, first_row, own = lax.optimization_barrier((cutoff, first_row, own))
    other = swap(own, 1)
    coulomb, other = lax.optimization_barrier((coulomb_slab(cutoff, first_row), other))
    flops = 2 * 2 * FIELDS * 3 * 8 * 256**3
    with jax.named_scope("forward_planes"):
        spectrum = call(
            forward_kernel,
            jax.ShapeDtypeStruct((8, CHUNK + ROWS, GRID), BF16),
            [pltpu.VMEM((2 * FIELDS, ROWS * PLANE, GRID), F32)],
            flops,
            operands=5,
        )(core, orbitals, theirs, own, other, tables)
    spectrum = exchange_slabs(spectrum)
    with jax.named_scope("coulomb_solve"):
        solved = call(
            solve_kernel,
            jax.ShapeDtypeStruct((8, FIELDS, ROWS, 2, ROWS, GRID), BF16),
            [pltpu.VMEM((ROWS * PAIR, GRID), F32)],
            flops,
            operands=3,
        )(kind.astype(jnp.int32).reshape(1), spectrum, coulomb, both_tables)
    solved = exchange_slabs(solved)
    slab = (2, ROWS, GRID, GRID)
    half = (HALF // 2, 2, GRID, GRID)
    with jax.named_scope("backward_planes"):
        exchange, passed, keep, send = call(
            backward_kernel,
            tuple(
                jax.ShapeDtypeStruct(shape, kind)
                for shape, kind in ((slab, F32), (slab, BF16), (half, F32), (half, BF16))
            ),
            [],
            flops,
            operands=6,
        )(core, solved, orbitals, theirs, own, other, tables)
    own, other, passed = total_terms(keep, send, passed)
    outs = jax.ShapeDtypeStruct((STEPS, ROWS, GRID, GRID), BF16)
    total = call(assemble, outs, [], 1 << 20, operands=2)(core, own, other)
    return exchange + passed.astype(F32), total


def solution(mesh):
    return jax.shard_map(
        shards,
        mesh=mesh,
        in_specs=(P("band", "ga", None, None), P(), P()),
        out_specs=(P("band", "ga", None, None), P(None, "ga", None, None)),
        check_vma=False,
    )
```
